256 devices in a mesh: coil: 32 (over z_hi, x, core), sect: 8 (over y, z_lo).
Axes of the slice: x: 4, y: 4, z: 8 (z_hi: 4, z_lo: 2; z = z_hi * 2 + z_lo), core: 2. Of those that a mesh axis runs over, the one named last changes fastest.
Arguments:
- measured: float32 [256, 32, 16, 2, 192], P(None, 'coil', 'sect'), may hold values from -6 to 6
- coil_maps: float32 [256, 32, 16, 2, 192], P(None, 'coil', 'sect'), may hold values from -0.75 to 0.75
- sampling: int32 [16, 192], P('sect'), may hold values 0 or 1
- conv_first: bfloat16 [64, 54], replicated, may hold values from -0.875 to 0.875
- bias_first: float32 [64], replicated, may hold values from -3 to 3
- conv_second: bfloat16 [54, 64], replicated, may hold values from -0.15625 to 0.15625
- bias_second: float32 [2], replicated, may hold values from -1.5 to 1.5
Outputs:
- recon: float32 [256, 16, 2, 192], P('coil', 'sect')
The draws below stay inside these ranges and needn't reach their ends.
Inputs may be any that keep to these rules, and one draw needn't show every extreme that they name: sampling[s, l] is 1 where phase-encoding column l of slice s was measured, else 0.
All inputs are finite; a program needn't handle non-finite values. No bound on the sum of `sampling` on one device may be relied on, other than what follows from the above.
Results may differ from the reference program's by a relative error of at most 0.0029.
Values may be sent and summed in bfloat16 or wider, within the bound.
A program may use at most 64 MiB of HBM per device.

```python
import jax
import jax.numpy as jnp
from jax import lax

H = 256
W = 192
C = 32
CH = 64
ITERS = 2
S = 16


def plant(entries, stream_key, smallest, top_value):
    place = [jax.random.randint(jax.random.fold_in(stream_key, axis), (), 0, length) for axis, length in enumerate(entries.shape)]
    longest = entries.shape.index(max(entries.shape))
    next_to = place[:longest] + [(place[longest] + 1) % entries.shape[longest]] + place[longest + 1:]
    return entries.at[tuple(place)].set(smallest).at[tuple(next_to)].set(top_value)


def level_of(key, shape, split, smallest, largest):
    level = 1.0
    for dim, blocks in split:
        heights = jax.random.uniform(jax.random.fold_in(jax.random.fold_in(key, 6), dim), (blocks,), jnp.float32, smallest / len(split), largest / len(split))
        level = level * jnp.repeat(jnp.exp(heights), shape[dim] // blocks).reshape((-1,) + (1,) * (len(shape) - 1 - dim))
    return level


def scatter_about(own_key, dims, width, reach, split=(), held_as=jnp.bfloat16):
    loudness = level_of(own_key, dims, split, -0.22, 0.18) if split else 1.0
    values = jax.random.normal(own_key, dims, jnp.float32) * width * loudness
    return jnp.minimum(jnp.maximum(values, -reach), reach).astype(held_as)


def setup_inputs(seed: int = 0) -> dict:
    key_list = jax.random.split(jax.random.key(seed), 8)
    measured = scatter_about(key_list[0], (H, C, S, 2, W), 1.0, 6.0, ((1, 32), (2, 8)), jnp.float32)
    coil_maps = scatter_about(key_list[1], (H, C, S, 2, W), 0.125, 0.75, ((1, 32), (2, 8)), jnp.float32)
    sampling = plant((jax.random.randint(key_list[2], (S, W), 0, 3) < 1).astype(jnp.int32), jax.random.fold_in(key_list[2], 1), 0, 1)
    conv_first = scatter_about(key_list[3], (CH, 54), 54 ** -0.5, 0.875)
    bias_first = scatter_about(key_list[4], (CH,), 0.5, 3.0, (), jnp.float32)
    conv_second = scatter_about(key_list[5], (54, CH), (27 * CH) ** -0.5, 0.15625)
    bias_second = scatter_about(key_list[6], (2,), 0.3, 1.5, (), jnp.float32)
    return dict(measured=measured, coil_maps=coil_maps, sampling=sampling, conv_first=conv_first, bias_first=bias_first, conv_second=conv_second, bias_second=bias_second)


step_size = 0.5


def stack_taps(padded, out_rows, out_slices, breadth):
    windows = []
    for first in range(3):
        for second in range(3):
            for third in range(3):
                windows.append(padded[first:first + out_rows, second:second + out_slices, :, third:third + breadth])
    return jnp.concatenate(windows, axis=2)


def tap_sum(taps, out_rows, out_slices, breadth):
    result = jnp.zeros((out_rows, out_slices, 2, breadth), jnp.float32)
    position = 0
    for first in range(3):
        for second in range(3):
            for third in range(3):
                result = result + taps[first:first + out_rows, second:second + out_slices, 2 * position:2 * position + 2, third:third + breadth]
                position = position + 1
    return result


def to_complex(array):
    return lax.complex(array[:, :, 0, :], array[:, :, 1, :]).transpose(1, 0, 2)


def pack_parts(real_part, imag_part):
    return jnp.stack([real_part, imag_part], axis=1).transpose(2, 0, 1, 3)


def reference(measured, coil_maps, sampling, conv_first, bias_first, conv_second, bias_second):
    weights = sampling.astype(jnp.float32)[:, None, :]

    def back_project(image_cplx, use_image):
        def one_coil(running, coil):
            maps = to_complex(lax.dynamic_index_in_dim(coil_maps, coil, 1, keepdims=False))
            data = to_complex(lax.dynamic_index_in_dim(measured, coil, 1, keepdims=False))
            if use_image:
                resid = weights * (jnp.fft.fft2(maps * image_cplx, norm="ortho") - data)
            else:
                resid = weights * data
            term = jnp.conj(maps) * jnp.fft.ifft2(resid, norm="ortho")
            return (running[0] + jnp.real(term), running[1] + jnp.imag(term)), None

        start = (jnp.zeros((S, H, W), jnp.float32), jnp.zeros((S, H, W), jnp.float32))
        final, unused = lax.scan(one_coil, start, jnp.arange(C, dtype=jnp.int32))
        return pack_parts(final[0], final[1])

    def regularize(damped):
        damped_half = damped.astype(jnp.bfloat16)
        padded = jnp.pad(damped_half, ((1, 1), (1, 1), (0, 0), (1, 1)))
        columns = stack_taps(padded, H, S, W).astype(jnp.float32)
        hidden = jnp.einsum("oc,rscw->rsow", conv_first.astype(jnp.float32), columns, precision=lax.Precision.HIGHEST)
        hidden = jax.nn.relu(hidden + bias_first[None, None, :, None]).astype(jnp.bfloat16)
        padded_hidden = jnp.pad(hidden, ((1, 1), (1, 1), (0, 0), (1, 1))).astype(jnp.float32)
        taps = jnp.einsum("tc,rscw->rstw", conv_second.astype(jnp.float32), padded_hidden, precision=lax.Precision.HIGHEST)
        update = tap_sum(taps, H, S, W) + bias_second[None, None, :, None]
        return damped + update

    image = back_project(None, False)
    for turn in range(ITERS):
        damped = image - step_size * back_project(to_complex(image), True)
        image = regularize(damped)
    return image
```

```python
import math

import jax
import jax.numpy as jnp
import ml_dtypes
import numpy as np
from jax import lax
from jax.experimental import pallas as pl
from jax.experimental.pallas import tpu as pltpu
from jax.sharding import PartitionSpec as P

ITERS = 2
STEP = 0.5
X_CHIPS = 4
W = 192
CH = 64
ROWS = 8
F32 = jnp.float32
BF16 = jnp.bfloat16
MESH = pl.DeviceIdType.MESH

PACKED = np.concatenate([np.arange(0, 128), np.arange(192, 320), np.arange(128, 192), np.arange(320, 384)])
OFFSETS = [(i, j) for i in (-1, 0, 1) for j in (-1, 0, 1) if (i, j) != (0, 0)]


def split_halves(table):
    high = table.astype(ml_dtypes.bfloat16)
    low = (table - high.astype(np.float64)).astype(ml_dtypes.bfloat16)
    return high, low


def dft(length):
    index = np.arange(length)
    angle = (index[:, None] * index[None, :] % length) * (2.0 * math.pi / length)
    return np.cos(angle) / math.sqrt(length), np.sin(angle) / math.sqrt(length)


def tables(height):
    cosine, sine = dft(W)
    column = np.block([[cosine, -sine], [sine, cosine]])[PACKED][:, PACKED]
    cosine, sine = dft(height)
    row = np.concatenate([cosine, sine], axis=1)
    pick_first = np.zeros((4, 54, 144), np.float32)
    pick_second = np.zeros((4, 72, 54), np.float32)
    for a in range(3):
        for b in range(3):
            for e in range(3):
                for q in range(2):
                    tap = 2 * (9 * a + 3 * b + e) + q
                    for s in range(4):
                        pick_first[s, tap, 48 * e + 16 * a + 2 * (s + b) + q] = 1.0
                        if 0 <= s - b < 2:
                            pick_second[s, 24 * a + 8 * e + 2 * (s - b) + q, tap] = 1.0
    repeat = np.tile(np.eye(CH, dtype=np.float32), (1, 4))
    as_half = lambda t: t.astype(ml_dtypes.bfloat16)
    return split_halves(column) + split_halves(row) + (as_half(pick_first), as_half(pick_second), as_half(repeat))


def dot(a, b, dims=((1,), (0,))):
    return lax.dot_general(a, b, (dims, ((), ())), preferred_element_type=F32)


def halves(value):
    high = value.astype(BF16)
    return high, (value - high.astype(F32)).astype(BF16)


def pack_rows(value):
    return jnp.concatenate([value[0:128], value[192:320], value[128:192], value[320:384]], axis=0)


def low_lanes(shape):
    return lax.broadcasted_iota(jnp.int32, shape, len(shape) - 1) < 64


def unpack(value):
    third = value[:, 256:384]
    low = low_lanes(third.shape)
    real = (value[:, 0:128], jnp.where(low, third, 0.0))
    imag = (value[:, 128:256], jnp.where(low, pltpu.roll(third, 64, 1), 0.0))
    return real, imag


def pack(real, imag):
    third = jnp.where(low_lanes(real[1].shape), real[1], pltpu.roll(imag[1], 64, 1))
    return jnp.concatenate([real[0], imag[0], third], axis=1)


def kernel(n, sections, meas_hbm, maps_hbm, th_hbm, tl_hbm, eh_hbm, el_hbm,
           samp_ref, first_ref, bias_first_ref, second_ref, bias_second_ref, pick_first_ref, pick_second_ref,
           repeat_ref, out_ref,
           meas, maps, th, tl, eh, el, masked, spread, outgoing, gathered, gathered_f, gathered_swap,
           part, got1, sum1, got2, sum2, got3, weight1, weight2, bias_full, edge_out, edge_in, grid_rows, grid_half,
           result, load_sem, maps_send, maps_recv, rs1_send, rs1_recv, rs2_send, rs2_recv, rs3_send, rs3_recv,
           edge_send, edge_recv):
    coil = lax.axis_index("coil")
    sect = lax.axis_index("sect")
    core = lax.rem(coil, 2)
    x_size = sum1.shape[2]
    z_size = sum1.shape[1]
    x = lax.rem(coil // 2, x_size)
    z = coil // (2 * x_size)

    loads = [
        pltpu.make_async_copy(src, dst, load_sem.at[i])
        for i, (src, dst) in enumerate(
            [(maps_hbm, maps), (meas_hbm, meas), (th_hbm, th), (tl_hbm, tl), (eh_hbm, eh), (el_hbm, el)]
        )
    ]
    for load in loads:
        load.start()

    barrier = pltpu.get_barrier_semaphore()

    def greet(d, carry):
        pl.semaphore_signal(barrier, inc=1, device_id=(lax.rem(coil + d, n), sect), device_id_type=MESH)
        return carry

    lax.fori_loop(1, n, greet, 0)
    for dc in (-1, 0, 1):
        for ds in (-1, 1):
            peer = (lax.rem(coil + dc + n, n), lax.rem(sect + ds + sections, sections))
            pl.semaphore_signal(barrier, inc=1, device_id=peer, device_id_type=MESH)

    loads[0].wait()
    turned = [pack_rows(maps[s]).T.reshape(n, ROWS, 384) for s in range(2)]
    outgoing[...] = jnp.concatenate(turned, axis=1).astype(BF16)
    gathered[coil] = outgoing[coil]
    pl.semaphore_wait(barrier, n - 1 + 6)

    def maps_copy(d):
        peer = lax.rem(coil + d, n)
        return pltpu.make_async_remote_copy(
            src_ref=outgoing.at[peer], dst_ref=gathered.at[coil], send_sem=maps_send.at[d], recv_sem=maps_recv.at[d],
            device_id=(peer, sect), device_id_type=MESH,
        )

    def send_maps(d, carry):
        maps_copy(d).start()
        return carry

    lax.fori_loop(1, n, send_maps, 0)

    loads[2].wait()
    loads[3].wait()
    for s in range(2):
        mask = samp_ref[s:s + 1, :].astype(F32)
        mask = jnp.concatenate([mask, jnp.zeros((1, 64), F32)], axis=1)
        tail = mask[:, 128:256]
        mask = jnp.concatenate([mask[:, 0:128], mask[:, 0:128], tail + pltpu.roll(tail, 64, 1)], axis=1)
        masked[s, 0] = (th[...].astype(F32) * mask).astype(BF16)
        masked[s, 1] = (tl[...].astype(F32) * mask).astype(BF16)

    loads[1].wait()
    loads[4].wait()
    loads[5].wait()
    copies1 = []
    for s in range(2):
        xh, xl = halves(pack_rows(meas[s]))
        column = dot(masked[s, 0], xh) + dot(masked[s, 0], xl) + dot(masked[s, 1], xh)
        zh, zl = halves(column)
        both = dot(zh, eh[...]) + dot(zl, eh[...]) + dot(zh, el[...])
        height = both.shape[1] // 2
        by_cos, by_sin = both[:, :height], both[:, height:]
        m = pack_rows(maps[s])
        terms = []
        for r0, i0, size in ((0, 128, 128), (256, 320, 64)):
            re, im = slice(r0, r0 + size), slice(i0, i0 + size)
            y_re = by_cos[re] - by_sin[im]
            y_im = by_cos[im] + by_sin[re]
            terms += [m[re] * y_re + m[im] * y_im, m[re] * y_im - m[im] * y_re]
        part[s] = jnp.concatenate(terms, axis=0).T.reshape(n // 2, 2, ROWS, 384)
        copy = pltpu.make_async_remote_copy(
            src_ref=part.at[s, :, 1 - core], dst_ref=got1.at[s], send_sem=rs1_send.at[s], recv_sem=rs1_recv.at[s],
            device_id=(coil + 1 - 2 * core, sect), device_id_type=MESH,
        )
        copy.start()
        copies1.append(copy)

    copies2 = []
    for s in range(2):
        copies1[s].wait_recv()
        sum1[s] = (part[s, :, core] + got1[s]).reshape(z_size, x_size, ROWS, 384)
        for d in range(1, x_size):
            to = lax.rem(x + d, x_size)
            copy = pltpu.make_async_remote_copy(
                src_ref=sum1.at[s, :, to], dst_ref=got2.at[s, d - 1],
                send_sem=rs2_send.at[s, d - 1], recv_sem=rs2_recv.at[s, d - 1],
                device_id=((z * x_size + to) * 2 + core, sect), device_id_type=MESH,
            )
            copy.start()
            copies2.append(copy)

    for s in range(2):
        last = ((1,), (1,))
        mh, ml = masked[s, 0], masked[s, 1]
        high, low = halves(dot(mh, mh, last) + dot(mh, ml, last) + dot(ml, mh, last))
        spread[s, 0] = high
        spread[s, 1] = low

    copies3 = []
    for s in range(2):
        total = sum1[s, :, x]
        for d in range(1, x_size):
            copies2[s * (x_size - 1) + d - 1].wait_recv()
            total = total + got2[s, d - 1]
        sum2[s] = total
        for d in range(1, z_size):
            to = lax.rem(z + d, z_size)
            copy = pltpu.make_async_remote_copy(
                src_ref=sum2.at[s, to], dst_ref=got3.at[s, d - 1],
                send_sem=rs3_send.at[s, d - 1], recv_sem=rs3_recv.at[s, d - 1],
                device_id=((to * x_size + x) * 2 + core, sect), device_id_type=MESH,
            )
            copy.start()
            copies3.append(copy)

    for s in range(4):
        weight1[64 * s:64 * s + 64] = dot(first_ref[...], pick_first_ref[s], ((0,), (0,))).astype(BF16)
    repeated = dot(second_ref[...], repeat_ref[...]).astype(BF16)
    of_slice = lax.broadcasted_iota(jnp.int32, (72, 256), 1) // 64
    second = jnp.zeros((72, 256), F32)
    for s in range(4):
        inside = jnp.logical_and(2 * sect - 1 + s >= 0, 2 * sect - 1 + s < 2 * sections)
        block = dot(pick_second_ref[s], repeated)
        second = second + jnp.where(jnp.logical_and(of_slice == s, inside), block, 0.0)
    weight2[...] = second.astype(BF16)
    diagonal = lax.broadcasted_iota(jnp.int32, (64, 64), 0) == lax.broadcasted_iota(jnp.int32, (64, 64), 1)
    bias_column = jnp.sum(jnp.where(diagonal, bias_first_ref[...], 0.0), axis=1, keepdims=True)
    for s in range(4):
        bias_full[64 * s:64 * s + 64] = jnp.broadcast_to(bias_column, (64, 256))
    grid_rows[...] = jnp.zeros_like(grid_rows)

    def wait_maps(d, carry):
        maps_copy(d).wait()
        return carry

    lax.fori_loop(1, n, wait_maps, 0)
    every = gathered[...].astype(F32)
    for s in range(2):
        mine = every[:, ROWS * s:ROWS * s + ROWS, :]
        gathered_f[s] = mine
        gathered_swap[s] = pltpu.roll(mine[:, :, 256:384].reshape(n * ROWS, 128), 64, 1).reshape(n, ROWS, 128)

    first_image = []
    for s in range(2):
        total = sum2[s, z]
        for d in range(1, z_size):
            copies3[s * (z_size - 1) + d - 1].wait_recv()
            total = total + got3[s, d - 1]
        first_image.append(total)

    lane = lax.broadcasted_iota(jnp.int32, (ROWS, 128), 1)
    low = lane < 64
    lanes_in = lax.broadcasted_iota(jnp.int32, (72, 256), 1) < W
    row_of_8 = lax.broadcasted_iota(jnp.int32, (ROWS, 256), 0)
    bias_rows = jnp.where(lax.rem(row_of_8, 2) == 0, bias_second_ref[0], bias_second_ref[1])
    image = first_image
    edge_copies = []
    for turn in range(ITERS):
        damped = []
        for s in range(2):
            v = image[s]
            va, vb, vc = v[:, 0:128], v[:, 128:256], v[:, 256:384]
            turned_c = pltpu.roll(vc, 64, 1)
            v_re = jnp.where(low, vc, turned_c)[None]
            v_im = jnp.where(low, -turned_c, vc)[None]
            ma, mb, mc = gathered_f[s, :, :, 0:128], gathered_f[s, :, :, 128:256], gathered_f[s, :, :, 256:384]
            ms = gathered_swap[s]
            va, vb = va[None], vb[None]
            pieces = [ma * va - mb * vb, ma * vb + mb * va, mc * v_re + ms * v_im]
            product = jnp.concatenate([p.reshape(n * ROWS, 128) for p in pieces], axis=1).astype(BF16)
            back = (dot(product, spread[s, 0]) + dot(product, spread[s, 1])).reshape(n, ROWS, 384)
            qa, qb, qc = back[:, :, 0:128], back[:, :, 128:256], back[:, :, 256:384]
            oa = jnp.sum(ma * qa + mb * qb, axis=0)
            ob = jnp.sum(ma * qb - mb * qa, axis=0)
            same = jnp.sum(mc * qc, axis=0)
            cross = jnp.sum(ms * qc, axis=0)
            oc = jnp.where(low, same + pltpu.roll(same, 64, 1), cross - pltpu.roll(cross, 64, 1))
            summed = jnp.concatenate([oa, ob, oc], axis=1)
            damped.append(v - STEP * (summed - first_image[s]))

        edge_out[turn] = jnp.concatenate(damped, axis=0).astype(BF16)
        copies = []
        for i, (dc, ds) in enumerate(OFFSETS):
            peer = (lax.rem(coil + dc + n, n), lax.rem(sect + ds + sections, sections))
            copy = pltpu.make_async_remote_copy(
                src_ref=edge_out.at[turn], dst_ref=edge_in.at[turn, i],
                send_sem=edge_send.at[turn, i], recv_sem=edge_recv.at[turn, i],
                device_id=peer, device_id_type=MESH,
            )
            copy.start()
            copies.append(copy)
        edge_copies += copies

        for dc, ds in [(0, 0)] + [(-i, -j) for i, j in OFFSETS]:
            if (dc, ds) == (0, 0):
                blocks = damped
            else:
                i = OFFSETS.index((-dc, -ds))
                copies[i].wait_recv()
                inside = jnp.logical_and(
                    jnp.logical_and(coil + dc >= 0, coil + dc < n),
                    jnp.logical_and(sect + ds >= 0, sect + ds < sections),
                )
                block = jnp.where(inside, edge_in[turn, i].astype(F32), 0.0)
                blocks = [block[0:ROWS], block[ROWS:2 * ROWS]]
            for s in range(2):
                for q, value in enumerate(unpack(blocks[s])):
                    k = 2 * (2 + 2 * ds + s) + q
                    for t in range(2):
                        if dc == 0:
                            grid_rows[t, pl.ds(32 + k, ROWS, stride=16), :] = value[t]
                        elif dc < 0:
                            grid_rows[t, k:k + 1, :] = value[t][ROWS - 2:ROWS - 1]
                            grid_rows[t, 16 + k:17 + k, :] = value[t][ROWS - 1:ROWS]
                        else:
                            grid_rows[t, 160 + k:161 + k, :] = value[t][0:1]
                            grid_rows[t, 176 + k:177 + k, :] = value[t][1:2]
        rows = jnp.concatenate([grid_rows[0], grid_rows[1]], axis=1)
        grid_half[0] = pltpu.roll(rows, 1, 1).astype(BF16)
        grid_half[1] = rows.astype(BF16)
        grid_half[2] = pltpu.roll(rows, 255, 1).astype(BF16)

        sums = [None] * ROWS
        for r in range(ROWS + 2):
            taps = jnp.concatenate([grid_half[e, 16 * r:16 * r + 48, :] for e in range(3)], axis=0)
            hidden = jnp.maximum(dot(weight1[...], taps) + bias_full[...], 0.0).astype(BF16)
            spots = jnp.where(lanes_in, dot(weight2[...], hidden), 0.0)
            if r == 0:
                spots = jnp.where(coil > 0, spots, 0.0)
            if r == ROWS + 1:
                spots = jnp.where(coil < n - 1, spots, 0.0)
            for a in range(3):
                if 0 <= r - a < ROWS:
                    piece = spots[24 * a:24 * a + 24]
                    sums[r - a] = piece if sums[r - a] is None else sums[r - a] + piece
        for r in range(ROWS):
            update = pltpu.roll(sums[r][0:8], 1, 1) + sums[r][8:16] + pltpu.roll(sums[r][16:24], 255, 1) + bias_rows
            for t in range(2):
                result[t, 8 * r:8 * r + 8, :] = update[:, 128 * t:128 * t + 128]

        image = []
        for s in range(2):
            update = [[result[t, pl.ds(2 * s + q, ROWS, stride=8), :] for t in range(2)] for q in range(2)]
            if turn < ITERS - 1:
                image.append(damped[s] + pack(*update))
            else:
                for q, value in enumerate(unpack(damped[s])):
                    for t in range(2):
                        result[t, pl.ds(2 * s + q, ROWS, stride=8), :] = value[t] + update[q][t]

    out_ref[:, 0:128] = result[0]
    out_ref[:, 128:256] = result[1]
    for copy in copies1 + copies2 + copies3 + edge_copies:
        copy.wait_send()


def per_device(n, sections, measured, coil_maps, sampling, conv_first, bias_first, conv_second, bias_second):
    height = measured.shape[0]
    by_columns = lambda t: t.transpose(1, 2, 3, 4, 0).reshape(2, 2 * W, height)
    consts = [jnp.asarray(t) for t in tables(height)]
    chips = n // 2
    x_size = min(X_CHIPS, chips // 2)
    z_size = chips // x_size
    vmem = pl.BlockSpec(memory_space=pltpu.VMEM)
    hbm = pl.BlockSpec(memory_space=pl.ANY)
    dma = pltpu.SemaphoreType.DMA
    out = pl.pallas_call(
        lambda *refs: kernel(n, sections, *refs),
        out_shape=jax.ShapeDtypeStruct((8 * ROWS, 256), F32),
        in_specs=[hbm] * 6 + [vmem] * 4 + [pl.BlockSpec(memory_space=pltpu.SMEM)] + [vmem] * 3,
        out_specs=vmem,
        scratch_shapes=[
            pltpu.VMEM((2, 384, height), F32),
            pltpu.VMEM((2, 384, height), F32),
            pltpu.VMEM((384, 384), BF16),
            pltpu.VMEM((384, 384), BF16),
            pltpu.VMEM((height, 2 * height), BF16),
            pltpu.VMEM((height, 2 * height), BF16),
            pltpu.VMEM((2, 2, 384, 384), BF16),
            pltpu.VMEM((2, 2, 384, 384), BF16),
            pltpu.VMEM((n, 2 * ROWS, 384), BF16),
            pltpu.VMEM((n, 2 * ROWS, 384), BF16),
            pltpu.VMEM((2, n, ROWS, 384), F32),
            pltpu.VMEM((2, n, ROWS, 128), F32),
            pltpu.VMEM((2, chips, 2, ROWS, 384), F32),
            pltpu.VMEM((2, chips, ROWS, 384), F32),
            pltpu.VMEM((2, z_size, x_size, ROWS, 384), F32),
            pltpu.VMEM((2, x_size - 1, z_size, ROWS, 384), F32),
            pltpu.VMEM((2, z_size, ROWS, 384), F32),
            pltpu.VMEM((2, z_size - 1, ROWS, 384), F32),
            pltpu.VMEM((256, 144), BF16),
            pltpu.VMEM((72, 256), BF16),
            pltpu.VMEM((256, 256), F32),
            pltpu.VMEM((ITERS, 2 * ROWS, 384), BF16),
            pltpu.VMEM((ITERS, 8, 2 * ROWS, 384), BF16),
            pltpu.VMEM((2, 192, 128), F32),
            pltpu.VMEM((3, 192, 256), BF16),
            pltpu.VMEM((2, 8 * ROWS, 128), F32),
            dma((6,)),
            dma((n,)),
            dma((n,)),
            dma((2,)),
            dma((2,)),
            dma((2, x_size - 1)),
            dma((2, x_size - 1)),
            dma((2, z_size - 1)),
            dma((2, z_size - 1)),
            dma((ITERS, 8)),
            dma((ITERS, 8)),
        ],
        compiler_params=pltpu.CompilerParams(
            collective_id=0, has_side_effects=True, vmem_limit_bytes=40 * 1024 * 1024
        ),
        name="reconstruct",
    )(
        by_columns(measured), by_columns(coil_maps), *consts[:4],
        sampling, conv_first.T, bias_first.reshape(1, CH), conv_second, bias_second, *consts[4:],
    )
    return out.reshape(ROWS, 8, 256)[:, :4, :W].reshape(ROWS, 2, 2, W)


def solution(mesh):
    n, sections = mesh.shape["coil"], mesh.shape["sect"]
    split = P(None, "coil", "sect", None, None)
    return jax.shard_map(
        lambda *args: per_device(n, sections, *args),
        mesh=mesh,
        in_specs=(split, split, P("sect", None), P(), P(), P(), P()),
        out_specs=P("coil", "sect", None, None),
        check_vma=False,
    )
```

```python
import math

import jax
import jax.numpy as jnp
import ml_dtypes
import numpy as np
from jax import lax
from jax.experimental import pallas as pl
from jax.experimental.pallas import tpu as pltpu
from jax.sharding import PartitionSpec as P

ITERS = 2
STEP = 0.5
X_CHIPS = 4
W = 192
CH = 64
BIAS_TAP = 48 + 16 + 12
ROWS = 8
F32 = jnp.float32
BF16 = jnp.bfloat16
MESH = pl.DeviceIdType.MESH

PACKED = np.concatenate([np.arange(0, 128), np.arange(192, 320), np.arange(128, 192), np.arange(320, 384)])
STRIPS = [(1, 1), (1, -1), (-1, 1), (-1, -1), (1, 0), (-1, 0)]


def split_halves(table):
    high = table.astype(ml_dtypes.bfloat16)
    low = (table - high.astype(np.float64)).astype(ml_dtypes.bfloat16)
    return high, low


def dft(length):
    index = np.arange(length)
    angle = (index[:, None] * index[None, :] % length) * (2.0 * math.pi / length)
    return np.cos(angle) / math.sqrt(length), np.sin(angle) / math.sqrt(length)


def tables(height):
    cosine, sine = dft(W)
    column = np.block([[cosine, -sine], [sine, cosine]])[PACKED][:, PACKED]
    cosine, sine = dft(height)
    row = np.concatenate([cosine, sine], axis=1)
    pick_first = np.zeros((4, 54, 144), np.float32)
    pick_second = np.zeros((4, 72, 54), np.float32)
    for a in range(3):
        for b in range(3):
            for e in range(3):
                for q in range(2):
                    tap = 2 * (9 * a + 3 * b + e) + q
                    for s in range(4):
                        pick_first[s, tap, 48 * e + 16 * a + 2 * (s + b) + q] = 1.0
                        if 0 <= s - b < 2:
                            pick_second[s, 24 * a + 8 * e + 2 * (s - b) + q, tap] = 1.0
    repeat = np.tile(np.eye(CH, dtype=np.float32), (1, 4))
    as_half = lambda t: t.astype(ml_dtypes.bfloat16)
    return split_halves(column) + split_halves(row) + (as_half(pick_first), as_half(pick_second), as_half(repeat))


def dot(a, b, dims=((1,), (0,))):
    return lax.dot_general(a, b, (dims, ((), ())), preferred_element_type=F32)


def halves(value):
    high = value.astype(BF16)
    return high, (value - high.astype(F32)).astype(BF16)


def pack_rows(value):
    return jnp.concatenate([value[0:128], value[192:320], value[128:192], value[320:384]], axis=0)


def low_lanes(shape):
    return lax.broadcasted_iota(jnp.int32, shape, len(shape) - 1) < 64


def unpack(value):
    third = value[:, 256:384]
    low = low_lanes(third.shape)
    real = (value[:, 0:128], jnp.where(low, third, 0.0))
    imag = (value[:, 128:256], jnp.where(low, pltpu.roll(third, 64, 1), 0.0))
    return real, imag


def pack(real, imag):
    third = jnp.where(low_lanes(real[1].shape), real[1], pltpu.roll(imag[1], 64, 1))
    return jnp.concatenate([real[0], imag[0], third], axis=1)


def kernel(n, sections, meas_hbm, maps_hbm, samp_hbm, th_hbm, tl_hbm, eh_hbm, el_hbm,
           first_hbm, bias_first_hbm, second_hbm, bias_second_hbm, pick_first_hbm, pick_second_hbm, repeat_hbm, out_ref,
           meas, maps, samp_ref, th, tl, eh, el,
           first_ref, bias_first_ref, second_ref, bias_second_ref, pick_first_ref, pick_second_ref, repeat_ref, masked, spread, outgoing, gathered, gathered_f, gathered_swap,
           part, got1, sum1, got2, sum2, got3, weight1, weight2, edge_out, edge_in, strip_rows, strip_out, strip_in, grid_rows, grid_half,
           result, load_sem, maps_send, maps_recv, rs1_send, rs1_recv, rs2_send, rs2_recv, rs3_send, rs3_recv,
           edge_send, edge_recv,
           strip_send, strip_recv):
    coil = lax.axis_index("coil")
    sect = lax.axis_index("sect")
    core = lax.rem(coil, 2)
    x_size = sum1.shape[2]
    z_size = sum1.shape[1]
    x = lax.rem(coil // 2, x_size)
    z = coil // (2 * x_size)

    loads = [
        pltpu.make_async_copy(src, dst, load_sem.at[i])
        for i, (src, dst) in enumerate(
            [
                (samp_hbm, samp_ref), (th_hbm, th), (tl_hbm, tl), (meas_hbm, meas), (eh_hbm, eh), (el_hbm, el),
                (maps_hbm, maps), (first_hbm, first_ref), (bias_first_hbm, bias_first_ref), (second_hbm, second_ref),
                (bias_second_hbm, bias_second_ref), (pick_first_hbm, pick_first_ref),
                (pick_second_hbm, pick_second_ref), (repeat_hbm, repeat_ref),
            ]
        )
    ]
    for load in loads:
        load.start()

    barrier = pltpu.get_barrier_semaphore()

    def greet(d, carry):
        pl.semaphore_signal(barrier, inc=1, device_id=(lax.rem(coil + d, n), sect), device_id_type=MESH)
        return carry

    lax.fori_loop(1, n, greet, 0)
    for dc in (-1, 0, 1):
        for ds in (-1, 1):
            peer = (lax.rem(coil + dc + n, n), lax.rem(sect + ds + sections, sections))
            pl.semaphore_signal(barrier, inc=1, device_id=peer, device_id_type=MESH)

    for load in loads[:3]:
        load.wait()
    for s in range(2):
        mask = samp_ref[s:s + 1, :].astype(F32)
        mask = jnp.concatenate([mask, jnp.zeros((1, 64), F32)], axis=1)
        tail = mask[:, 128:256]
        mask = jnp.concatenate([mask[:, 0:128], mask[:, 0:128], tail + pltpu.roll(tail, 64, 1)], axis=1)
        masked[s, 0] = (th[...].astype(F32) * mask).astype(BF16)
        masked[s, 1] = (tl[...].astype(F32) * mask).astype(BF16)

    for load in loads[3:7]:
        load.wait()
    copies1 = []
    for s in range(2):
        xh, xl = halves(pack_rows(meas[s]))
        column = dot(masked[s, 0], xh) + dot(masked[s, 0], xl) + dot(masked[s, 1], xh)
        zh, zl = halves(column)
        both = dot(zh, eh[...]) + dot(zl, eh[...]) + dot(zh, el[...])
        height = both.shape[1] // 2
        by_cos, by_sin = both[:, :height], both[:, height:]
        m = pack_rows(maps[s])
        terms = []
        for r0, i0, size in ((0, 128, 128), (256, 320, 64)):
            re, im = slice(r0, r0 + size), slice(i0, i0 + size)
            y_re = by_cos[re] - by_sin[im]
            y_im = by_cos[im] + by_sin[re]
            terms += [m[re] * y_re + m[im] * y_im, m[re] * y_im - m[im] * y_re]
        part[s] = jnp.concatenate(terms, axis=0).T.reshape(n // 2, 2, ROWS, 384)
        if s == 0:
            pl.semaphore_wait(barrier, n - 1 + 6)
        copy = pltpu.make_async_remote_copy(
            src_ref=part.at[s, :, 1 - core], dst_ref=got1.at[s], send_sem=rs1_send.at[s], recv_sem=rs1_recv.at[s],
            device_id=(coil + 1 - 2 * core, sect), device_id_type=MESH,
        )
        copy.start()
        copies1.append(copy)

    turned = [pack_rows(maps[s]).T.reshape(n, ROWS, 384) for s in range(2)]
    outgoing[...] = jnp.concatenate(turned, axis=1).astype(BF16)
    gathered[coil] = outgoing[coil]

    def maps_copy(d):
        peer = lax.rem(coil + d, n)
        return pltpu.make_async_remote_copy(
            src_ref=outgoing.at[peer], dst_ref=gathered.at[coil], send_sem=maps_send.at[d], recv_sem=maps_recv.at[d],
            device_id=(peer, sect), device_id_type=MESH,
        )

    def send_maps(d, carry):
        maps_copy(d).start()
        return carry

    lax.fori_loop(1, n, send_maps, 0)

    copies2 = []
    for s in range(2):
        copies1[s].wait_recv()
        sum1[s] = (part[s, :, core] + got1[s]).reshape(z_size, x_size, ROWS, 384)
        for d in range(1, x_size):
            to = lax.rem(x + d, x_size)
            copy = pltpu.make_async_remote_copy(
                src_ref=sum1.at[s, :, to], dst_ref=got2.at[s, d - 1],
                send_sem=rs2_send.at[s, d - 1], recv_sem=rs2_recv.at[s, d - 1],
                device_id=((z * x_size + to) * 2 + core, sect), device_id_type=MESH,
            )
            copy.start()
            copies2.append(copy)

    for s in range(2):
        last = ((1,), (1,))
        mh, ml = masked[s, 0], masked[s, 1]
        high, low = halves(dot(mh, mh, last) + dot(mh, ml, last) + dot(ml, mh, last))
        spread[s, 0] = high
        spread[s, 1] = low

    copies3 = []
    for s in range(2):
        total = sum1[s, :, x]
        for d in range(1, x_size):
            copies2[s * (x_size - 1) + d - 1].wait_recv()
            total = total + got2[s, d - 1]
        sum2[s] = total
        for d in range(1, z_size):
            to = lax.rem(z + d, z_size)
            copy = pltpu.make_async_remote_copy(
                src_ref=sum2.at[s, to], dst_ref=got3.at[s, d - 1],
                send_sem=rs3_send.at[s, d - 1], recv_sem=rs3_recv.at[s, d - 1],
                device_id=((to * x_size + x) * 2 + core, sect), device_id_type=MESH,
            )
            copy.start()
            copies3.append(copy)

    for load in loads[7:]:
        load.wait()
    repeated = dot(second_ref[...], repeat_ref[...]).astype(BF16)
    of_slice = lax.broadcasted_iota(jnp.int32, (72, 256), 1) // 64
    second = jnp.zeros((72, 256), F32)
    for s in range(4):
        inside = jnp.logical_and(2 * sect - 1 + s >= 0, 2 * sect - 1 + s < 2 * sections)
        block = dot(pick_second_ref[s], repeated)
        second = second + jnp.where(jnp.logical_and(of_slice == s, inside), block, 0.0)
    weight2[...] = second.astype(BF16)
    diagonal = lax.broadcasted_iota(jnp.int32, (64, 64), 0) == lax.broadcasted_iota(jnp.int32, (64, 64), 1)
    bias_column = jnp.sum(jnp.where(diagonal, bias_first_ref[...], 0.0), axis=1, keepdims=True)
    bias_high = bias_column.astype(BF16).astype(F32)
    bias_rest = bias_column - bias_high
    bias_middle = bias_rest.astype(BF16).astype(F32)
    spot = lax.broadcasted_iota(jnp.int32, (64, 144), 1)
    bias_taps = jnp.where(spot == BIAS_TAP, bias_high, 0.0)
    bias_taps = jnp.where(spot == BIAS_TAP + 1, bias_middle, bias_taps)
    bias_taps = jnp.where(spot == BIAS_TAP + 2, bias_rest - bias_middle, bias_taps)
    for s in range(4):
        block = dot(first_ref[...], pick_first_ref[s], ((0,), (0,)))
        weight1[64 * s:64 * s + 64] = (block + bias_taps).astype(BF16)
    place = lax.rem(lax.broadcasted_iota(jnp.int32, (192, 128), 0), 16)
    for t in range(2):
        grid_rows[t] = jnp.where(jnp.logical_and(place >= 12, place < 15), 1.0, 0.0)

    def wait_maps(d, carry):
        maps_copy(d).wait_recv()
        return carry

    lax.fori_loop(1, n, wait_maps, 0)
    every = gathered[...].astype(F32)
    for s in range(2):
        mine = every[:, ROWS * s:ROWS * s + ROWS, :]
        gathered_f[s] = mine
        gathered_swap[s] = pltpu.roll(mine[:, :, 256:384].reshape(n * ROWS, 128), 64, 1).reshape(n, ROWS, 128)

    first_image = []
    for s in range(2):
        total = sum2[s, z]
        for d in range(1, z_size):
            copies3[s * (z_size - 1) + d - 1].wait_recv()
            total = total + got3[s, d - 1]
        first_image.append(total)

    lane = lax.broadcasted_iota(jnp.int32, (ROWS, 128), 1)
    low = lane < 64
    lanes_in = lax.broadcasted_iota(jnp.int32, (72, 256), 1) < W
    row_of_8 = lax.broadcasted_iota(jnp.int32, (ROWS, 256), 0)
    bias_rows = jnp.where(lax.rem(row_of_8, 2) == 0, bias_second_ref[0:1, 0:1], bias_second_ref[0:1, 1:2])
    image = first_image
    for turn in range(ITERS):
        damped = []
        for s in range(2):
            v = image[s]
            va, vb, vc = v[:, 0:128], v[:, 128:256], v[:, 256:384]
            turned_c = pltpu.roll(vc, 64, 1)
            v_re = jnp.where(low, vc, turned_c)[None]
            v_im = jnp.where(low, -turned_c, vc)[None]
            ma, mb, mc = gathered_f[s, :, :, 0:128], gathered_f[s, :, :, 128:256], gathered_f[s, :, :, 256:384]
            ms = gathered_swap[s]
            va, vb = va[None], vb[None]
            pieces = [ma * va - mb * vb, ma * vb + mb * va, mc * v_re + ms * v_im]
            product = jnp.concatenate([p.reshape(n * ROWS, 128) for p in pieces], axis=1).astype(BF16)
            back = (dot(product, spread[s, 0]) + dot(product, spread[s, 1])).reshape(n, ROWS, 384)
            qa, qb, qc = back[:, :, 0:128], back[:, :, 128:256], back[:, :, 256:384]
            oa = jnp.sum(ma * qa + mb * qb, axis=0)
            ob = jnp.sum(ma * qb - mb * qa, axis=0)
            same = jnp.sum(mc * qc, axis=0)
            cross = jnp.sum(ms * qc, axis=0)
            oc = jnp.where(low, same + pltpu.roll(same, 64, 1), cross - pltpu.roll(cross, 64, 1))
            summed = jnp.concatenate([oa, ob, oc], axis=1)
            damped.append(v - STEP * (summed - first_image[s]))

        parts = [unpack(damped[s]) for s in range(2)]
        for side, top in enumerate((ROWS - 2, 0)):
            for s in range(2):
                for q in range(2):
                    for t in range(2):
                        for h in range(2):
                            row = 8 * t + 4 * h + 2 * s + q
                            strip_rows[side, row:row + 1, :] = parts[s][q][t][top + h:top + h + 1]
            strip_out[turn, side] = strip_rows[side].astype(BF16)
        strips = []
        for i, (dc, ds) in enumerate(STRIPS):
            peer = (lax.rem(coil + dc + n, n), lax.rem(sect + ds + sections, sections))
            copy = pltpu.make_async_remote_copy(
                src_ref=strip_out.at[turn, 0 if dc > 0 else 1], dst_ref=strip_in.at[turn, i],
                send_sem=strip_send.at[turn, i], recv_sem=strip_recv.at[turn, i],
                device_id=peer, device_id_type=MESH,
            )
            if ds == 0 and i == 4:
                edge_out[turn] = jnp.concatenate(damped, axis=0).astype(BF16)
                sides = []
                for k, step in enumerate((1, -1)):
                    across = pltpu.make_async_remote_copy(
                        src_ref=edge_out.at[turn], dst_ref=edge_in.at[turn, k],
                        send_sem=edge_send.at[turn, k], recv_sem=edge_recv.at[turn, k],
                        device_id=(coil, lax.rem(sect + step + sections, sections)), device_id_type=MESH,
                    )
                    across.start()
                    sides.append(across)
            copy.start()
            strips.append(copy)

        def place_slices(values, ds):
            for s in range(2):
                for q in range(2):
                    for t in range(2):
                        grid_rows[t, pl.ds(32 + 2 * (2 + 2 * ds + s) + q, ROWS, stride=16), :] = values[s][q][t]

        def halve(first, last):
            rows = jnp.concatenate([grid_rows[0, first:last], grid_rows[1, first:last]], axis=1)
            grid_half[0, first:last] = pltpu.roll(rows, 1, 1).astype(BF16)
            grid_half[1, first:last] = rows.astype(BF16)
            grid_half[2, first:last] = pltpu.roll(rows, 255, 1).astype(BF16)

        def spots_of(r):
            taps = jnp.concatenate([grid_half[e, 16 * r:16 * r + 48, :] for e in range(3)], axis=0)
            hidden = jnp.maximum(dot(weight1[...], taps), 0.0).astype(BF16)
            spots = jnp.where(lanes_in, dot(weight2[...], hidden), 0.0)
            if r == 0:
                spots = jnp.where(coil > 0, spots, 0.0)
            if r == ROWS + 1:
                spots = jnp.where(coil < n - 1, spots, 0.0)
            return spots

        place_slices(parts, 0)
        if turn == 0:
            for copy in copies1 + copies2 + copies3:
                copy.wait_send()

            def wait_sent(d, carry):
                maps_copy(d).wait_send()
                return carry

            lax.fori_loop(1, n, wait_sent, 0)
        for k, step in enumerate((1, -1)):
            sides[k].wait_recv()
            inside = jnp.logical_and(sect - step >= 0, sect - step < sections)
            block = jnp.where(inside, edge_in[turn, k].astype(F32), 0.0)
            place_slices([unpack(block[0:ROWS]), unpack(block[ROWS:2 * ROWS])], -step)
        halve(32, 160)
        spots = {r: spots_of(r) for r in range(2, ROWS)}

        for i, (dc, ds) in reversed(list(enumerate(STRIPS))):
            strips[i].wait_recv()
            inside = jnp.logical_and(
                jnp.logical_and(coil - dc >= 0, coil - dc < n),
                jnp.logical_and(sect - ds >= 0, sect - ds < sections),
            )
            block = jnp.where(inside, strip_in[turn, i].astype(F32), 0.0)
            for t in range(2):
                for h in range(2):
                    to = (0 if dc > 0 else 160) + 16 * h + 2 * (2 - 2 * ds)
                    grid_rows[t, to:to + 4, :] = block[8 * t + 4 * h:8 * t + 4 * h + 4]
        halve(0, 32)
        halve(160, 192)
        for r in (0, 1, ROWS, ROWS + 1):
            spots[r] = spots_of(r)

        for r in range(ROWS):
            taps = spots[r][0:24] + spots[r + 1][24:48] + spots[r + 2][48:72]
            update = pltpu.roll(taps[0:8], 1, 1) + taps[8:16] + pltpu.roll(taps[16:24], 255, 1) + bias_rows
            for t in range(2):
                result[t, 4 * r:4 * r + 4, :] = update[0:4, 128 * t:128 * t + 128]
        for copy in sides + strips:
            copy.wait_send()

        image = []
        for s in range(2):
            update = [[result[t, pl.ds(2 * s + q, ROWS, stride=4), :] for t in range(2)] for q in range(2)]
            if turn < ITERS - 1:
                image.append(damped[s] + pack(*update))
            else:
                for q, value in enumerate(parts[s]):
                    for t in range(2):
                        result[t, pl.ds(2 * s + q, ROWS, stride=4), :] = value[t] + update[q][t]

    for r in range(ROWS):
        for s in range(2):
            rows = slice(4 * r + 2 * s, 4 * r + 2 * s + 2)
            out_ref[r, s, :, 0:128] = result[0, rows]
            out_ref[r, s, :, 128:W] = result[1, rows, 0:W - 128]


def per_device(n, sections, measured, coil_maps, sampling, conv_first, bias_first, conv_second, bias_second):
    height = measured.shape[0]
    by_columns = lambda t: t.transpose(1, 2, 3, 4, 0).reshape(2, 2 * W, height)
    consts = [jnp.asarray(t) for t in tables(height)]
    chips = n // 2
    x_size = min(X_CHIPS, chips // 2)
    z_size = chips // x_size
    dma = pltpu.SemaphoreType.DMA
    out = pl.pallas_call(
        lambda *refs: kernel(n, sections, *refs),
        out_shape=pltpu.VMEM((ROWS, 2, 2, W), F32),
        in_specs=[pl.BlockSpec(memory_space=pl.ANY)] * 14,
        out_specs=pl.BlockSpec(memory_space=pltpu.VMEM),
        scratch_shapes=[
            pltpu.VMEM((2, 384, height), F32),
            pltpu.VMEM((2, 384, height), F32),
            pltpu.VMEM((2, W), jnp.int32),
            pltpu.VMEM((384, 384), BF16),
            pltpu.VMEM((384, 384), BF16),
            pltpu.VMEM((height, 2 * height), BF16),
            pltpu.VMEM((height, 2 * height), BF16),
            pltpu.VMEM((54, CH), BF16),
            pltpu.VMEM((1, CH), F32),
            pltpu.VMEM((54, CH), BF16),
            pltpu.VMEM((1, 2), F32),
            pltpu.VMEM((4, 54, 144), BF16),
            pltpu.VMEM((4, 72, 54), BF16),
            pltpu.VMEM((CH, 256), BF16),
            pltpu.VMEM((2, 2, 384, 384), BF16),
            pltpu.VMEM((2, 2, 384, 384), BF16),
            pltpu.VMEM((n, 2 * ROWS, 384), BF16),
            pltpu.VMEM((n, 2 * ROWS, 384), BF16),
            pltpu.VMEM((2, n, ROWS, 384), F32),
            pltpu.VMEM((2, n, ROWS, 128), F32),
            pltpu.VMEM((2, chips, 2, ROWS, 384), F32),
            pltpu.VMEM((2, chips, ROWS, 384), F32),
            pltpu.VMEM((2, z_size, x_size, ROWS, 384), F32),
            pltpu.VMEM((2, x_size - 1, z_size, ROWS, 384), F32),
            pltpu.VMEM((2, z_size, ROWS, 384), F32),
            pltpu.VMEM((2, z_size - 1, ROWS, 384), F32),
            pltpu.VMEM((256, 144), BF16),
            pltpu.VMEM((72, 256), BF16),
            pltpu.VMEM((ITERS, 2 * ROWS, 384), BF16),
            pltpu.VMEM((ITERS, 2, 2 * ROWS, 384), BF16),
            pltpu.VMEM((2, 16, 128), F32),
            pltpu.VMEM((ITERS, 2, 16, 128), BF16),
            pltpu.VMEM((ITERS, 6, 16, 128), BF16),
            pltpu.VMEM((2, 192, 128), F32),
            pltpu.VMEM((3, 192, 256), BF16),
            pltpu.VMEM((2, 4 * ROWS, 128), F32),
            dma((14,)),
            dma((n,)),
            dma((n,)),
            dma((2,)),
            dma((2,)),
            dma((2, x_size - 1)),
            dma((2, x_size - 1)),
            dma((2, z_size - 1)),
            dma((2, z_size - 1)),
            dma((ITERS, 2)),
            dma((ITERS, 2)),
            dma((ITERS, 6)),
            dma((ITERS, 6)),
        ],
        compiler_params=pltpu.CompilerParams(
            collective_id=0, has_side_effects=True, vmem_limit_bytes=60 * 1024 * 1024
        ),
        name="reconstruct",
    )(
        by_columns(measured), by_columns(coil_maps), sampling, *consts[:4],
        conv_first.T, bias_first.reshape(1, CH), conv_second, bias_second.reshape(1, 2), *consts[4:],
    )
    return out


def solution(mesh):
    n, sections = mesh.shape["coil"], mesh.shape["sect"]
    split = P(None, "coil", "sect", None, None)
    return jax.shard_map(
        lambda *args: per_device(n, sections, *args),
        mesh=mesh,
        in_specs=(split, split, P("sect", None), P(), P(), P(), P()),
        out_specs=P("coil", "sect", None, None),
        check_vma=False,
    )
```

```python
import math

import jax
import jax.numpy as jnp
import ml_dtypes
import numpy as np
from jax import lax
from jax.experimental import pallas as pl
from jax.experimental.pallas import tpu as pltpu
from jax.sharding import PartitionSpec as P

ITERS = 2
STEP = 0.5
X_CHIPS = 4
W = 192
CH = 64
BIAS_TAP = 48 + 16 + 12
ROWS = 8
F32 = jnp.float32
BF16 = jnp.bfloat16
MESH = pl.DeviceIdType.MESH

PACKED = np.concatenate([np.arange(0, 128), np.arange(192, 320), np.arange(128, 192), np.arange(320, 384)])
STRIPS = [(1, 1), (1, -1), (-1, 1), (-1, -1), (1, 0), (-1, 0)]


def split_halves(table):
    high = table.astype(ml_dtypes.bfloat16)
    low = (table - high.astype(np.float64)).astype(ml_dtypes.bfloat16)
    return high, low


def dft(length):
    index = np.arange(length)
    angle = (index[:, None] * index[None, :] % length) * (2.0 * math.pi / length)
    return np.cos(angle) / math.sqrt(length), np.sin(angle) / math.sqrt(length)


def tables(height):
    cosine, sine = dft(W)
    column = np.block([[cosine, -sine], [sine, cosine]])[PACKED][:, PACKED]
    cosine, sine = dft(height)
    row = np.concatenate([cosine, sine], axis=1)
    pick_first = np.zeros((4, 54, 144), np.float32)
    pick_second = np.zeros((4, 72, 54), np.float32)
    for a in range(3):
        for b in range(3):
            for e in range(3):
                for q in range(2):
                    tap = 2 * (9 * a + 3 * b + e) + q
                    for s in range(4):
                        pick_first[s, tap, 48 * e + 16 * a + 2 * (s + b) + q] = 1.0
                        if 0 <= s - b < 2:
                            pick_second[s, 24 * a + 8 * e + 2 * (s - b) + q, tap] = 1.0
    repeat = np.tile(np.eye(CH, dtype=np.float32), (1, 4))
    as_half = lambda t: t.astype(ml_dtypes.bfloat16)
    return split_halves(column) + split_halves(row) + (as_half(pick_first), as_half(pick_second), as_half(repeat))


def dot(a, b, dims=((1,), (0,))):
    return lax.dot_general(a, b, (dims, ((), ())), preferred_element_type=F32)


def halves(value):
    high = value.astype(BF16)
    return high, (value - high.astype(F32)).astype(BF16)


def pack_rows(value):
    return jnp.concatenate([value[0:128], value[192:320], value[128:192], value[320:384]], axis=0)


def low_lanes(shape):
    return lax.broadcasted_iota(jnp.int32, shape, len(shape) - 1) < 64


def unpack(value):
    third = value[:, 256:384]
    low = low_lanes(third.shape)
    real = (value[:, 0:128], jnp.where(low, third, 0.0))
    imag = (value[:, 128:256], jnp.where(low, pltpu.roll(third, 64, 1), 0.0))
    return real, imag


def pack(real, imag):
    third = jnp.where(low_lanes(real[1].shape), real[1], pltpu.roll(imag[1], 64, 1))
    return jnp.concatenate([real[0], imag[0], third], axis=1)


def kernel(n, sections, meas_hbm, maps_hbm, samp_hbm, th_hbm, tl_hbm, eh_hbm, el_hbm,
           first_hbm, bias_first_hbm, second_hbm, bias_second_hbm, pick_first_hbm, pick_second_hbm, repeat_hbm, out_ref,
           meas, maps, samp_ref, th, tl, eh, el,
           first_ref, bias_first_ref, second_ref, bias_second_ref, pick_first_ref, pick_second_ref, repeat_ref, masked, spread, outgoing, gathered, gathered_f, gathered_swap,
           part, got1, sum1, got2, sum2, got3, weight1, weight2, edge_out, edge_in, strip_rows, strip_out, strip_in, grid_rows, grid_half,
           result, load_sem, maps_send, maps_recv, rs1_send, rs1_recv, rs2_send, rs2_recv, rs3_send, rs3_recv,
           edge_send, edge_recv,
           strip_send, strip_recv):
    coil = lax.axis_index("coil")
    sect = lax.axis_index("sect")
    core = lax.rem(coil, 2)
    x_size = sum1.shape[2]
    z_size = sum1.shape[1]
    x = lax.rem(coil // 2, x_size)
    z = coil // (2 * x_size)

    loads = [
        pltpu.make_async_copy(src, dst, load_sem.at[i])
        for i, (src, dst) in enumerate(
            [
                (samp_hbm, samp_ref), (th_hbm, th), (tl_hbm, tl), (meas_hbm, meas), (eh_hbm, eh), (el_hbm, el),
                (maps_hbm, maps), (first_hbm, first_ref), (bias_first_hbm, bias_first_ref), (second_hbm, second_ref),
                (bias_second_hbm, bias_second_ref), (pick_first_hbm, pick_first_ref),
                (pick_second_hbm, pick_second_ref), (repeat_hbm, repeat_ref),
            ]
        )
    ]
    for load in loads:
        load.start()

    barrier = pltpu.get_barrier_semaphore()

    def greet(d, carry):
        pl.semaphore_signal(barrier, inc=1, device_id=(lax.rem(coil + d, n), sect), device_id_type=MESH)
        return carry

    lax.fori_loop(1, n, greet, 0)
    for dc in (-1, 0, 1):
        for ds in (-1, 1):
            peer = (lax.rem(coil + dc + n, n), lax.rem(sect + ds + sections, sections))
            pl.semaphore_signal(barrier, inc=1, device_id=peer, device_id_type=MESH)

    for load in loads[:3]:
        load.wait()
    for s in range(2):
        mask = samp_ref[s:s + 1, :].astype(F32)
        mask = jnp.concatenate([mask, jnp.zeros((1, 64), F32)], axis=1)
        tail = mask[:, 128:256]
        mask = jnp.concatenate([mask[:, 0:128], mask[:, 0:128], tail + pltpu.roll(tail, 64, 1)], axis=1)
        high = (th[...].astype(F32) * mask).astype(BF16)
        masked[s, :, 0:384] = high
        masked[s, :, 384:768] = (tl[...].astype(F32) * mask).astype(BF16)
        masked[s, :, 768:1152] = high

    for load in loads[3:7]:
        load.wait()
    copies1 = []
    columns = []
    for s in range(2):
        xh, xl = halves(pack_rows(meas[s]))
        columns.append(dot(masked[s], jnp.concatenate([xh, xh, xl], axis=0)))
    planes = []
    for s in range(2):
        zh, zl = halves(columns[s])
        planes.append(dot(jnp.concatenate([zh, zl, zh], axis=1), jnp.concatenate([eh[...], eh[...], el[...]], axis=0)))
    for s in range(2):
        both = planes[s]
        height = both.shape[1] // 2
        by_cos, by_sin = both[:, :height], both[:, height:]
        m = pack_rows(maps[s])
        terms = []
        for r0, i0, size in ((0, 128, 128), (256, 320, 64)):
            re, im = slice(r0, r0 + size), slice(i0, i0 + size)
            y_re = by_cos[re] - by_sin[im]
            y_im = by_cos[im] + by_sin[re]
            terms += [m[re] * y_re + m[im] * y_im, m[re] * y_im - m[im] * y_re]
        part[s] = jnp.concatenate(terms, axis=0).T.reshape(n // 2, 2, ROWS, 384)
        if s == 0:
            pl.semaphore_wait(barrier, n - 1 + 6)
        copy = pltpu.make_async_remote_copy(
            src_ref=part.at[s, :, 1 - core], dst_ref=got1.at[s], send_sem=rs1_send.at[s], recv_sem=rs1_recv.at[s],
            device_id=(coil + 1 - 2 * core, sect), device_id_type=MESH,
        )
        copy.start()
        copies1.append(copy)

    turned = [pack_rows(maps[s]).T.reshape(n, ROWS, 384) for s in range(2)]
    outgoing[...] = jnp.concatenate(turned, axis=1).astype(BF16)
    gathered[coil] = outgoing[coil]

    def maps_copy(d):
        peer = lax.rem(coil + d, n)
        return pltpu.make_async_remote_copy(
            src_ref=outgoing.at[peer], dst_ref=gathered.at[coil], send_sem=maps_send.at[d], recv_sem=maps_recv.at[d],
            device_id=(peer, sect), device_id_type=MESH,
        )

    def send_maps(d, carry):
        maps_copy(d).start()
        return carry

    lax.fori_loop(1, n, send_maps, 0)

    copies2 = []
    for s in range(2):
        copies1[s].wait_recv()
        sum1[s] = (part[s, :, core] + got1[s]).reshape(z_size, x_size, ROWS, 384)
        for d in range(1, x_size):
            to = lax.rem(x + d, x_size)
            copy = pltpu.make_async_remote_copy(
                src_ref=sum1.at[s, :, to], dst_ref=got2.at[s, d - 1],
                send_sem=rs2_send.at[s, d - 1], recv_sem=rs2_recv.at[s, d - 1],
                device_id=((z * x_size + to) * 2 + core, sect), device_id_type=MESH,
            )
            copy.start()
            copies2.append(copy)

    for s in range(2):
        last = ((1,), (1,))
        mh, ml = masked[s, :, 0:384], masked[s, :, 384:768]
        high, low = halves(dot(masked[s], jnp.concatenate([mh, mh, ml], axis=1), last))
        spread[s, 0:384] = high
        spread[s, 384:768] = low

    copies3 = []
    for s in range(2):
        total = sum1[s, :, x]
        for d in range(1, x_size):
            copies2[s * (x_size - 1) + d - 1].wait_recv()
            total = total + got2[s, d - 1]
        sum2[s] = total
        for d in range(1, z_size):
            to = lax.rem(z + d, z_size)
            copy = pltpu.make_async_remote_copy(
                src_ref=sum2.at[s, to], dst_ref=got3.at[s, d - 1],
                send_sem=rs3_send.at[s, d - 1], recv_sem=rs3_recv.at[s, d - 1],
                device_id=((to * x_size + x) * 2 + core, sect), device_id_type=MESH,
            )
            copy.start()
            copies3.append(copy)

    for load in loads[7:]:
        load.wait()
    repeated = dot(second_ref[...], repeat_ref[...]).astype(BF16)
    of_slice = lax.broadcasted_iota(jnp.int32, (72, 256), 1) // 64
    second = jnp.zeros((72, 256), F32)
    for s in range(4):
        inside = jnp.logical_and(2 * sect - 1 + s >= 0, 2 * sect - 1 + s < 2 * sections)
        block = dot(pick_second_ref[s], repeated)
        second = second + jnp.where(jnp.logical_and(of_slice == s, inside), block, 0.0)
    weight2[...] = second.astype(BF16)
    diagonal = lax.broadcasted_iota(jnp.int32, (64, 64), 0) == lax.broadcasted_iota(jnp.int32, (64, 64), 1)
    bias_column = jnp.sum(jnp.where(diagonal, bias_first_ref[...], 0.0), axis=1, keepdims=True)
    bias_high = bias_column.astype(BF16).astype(F32)
    bias_rest = bias_column - bias_high
    bias_middle = bias_rest.astype(BF16).astype(F32)
    spot = lax.broadcasted_iota(jnp.int32, (64, 144), 1)
    bias_taps = jnp.where(spot == BIAS_TAP, bias_high, 0.0)
    bias_taps = jnp.where(spot == BIAS_TAP + 1, bias_middle, bias_taps)
    bias_taps = jnp.where(spot == BIAS_TAP + 2, bias_rest - bias_middle, bias_taps)
    for s in range(4):
        block = dot(first_ref[...], pick_first_ref[s], ((0,), (0,)))
        weight1[64 * s:64 * s + 64] = (block + bias_taps).astype(BF16)
    place = lax.rem(lax.broadcasted_iota(jnp.int32, (192, 128), 0), 16)
    for t in range(2):
        grid_rows[t] = jnp.where(jnp.logical_and(place >= 12, place < 15), 1.0, 0.0)

    def wait_maps(d, carry):
        maps_copy(d).wait_recv()
        return carry

    lax.fori_loop(1, n, wait_maps, 0)
    every = gathered[...].astype(F32)
    for s in range(2):
        mine = every[:, ROWS * s:ROWS * s + ROWS, :]
        gathered_f[s] = mine
        gathered_swap[s] = pltpu.roll(mine[:, :, 256:384].reshape(n * ROWS, 128), 64, 1).reshape(n, ROWS, 128)

    first_image = []
    for s in range(2):
        total = sum2[s, z]
        for d in range(1, z_size):
            copies3[s * (z_size - 1) + d - 1].wait_recv()
            total = total + got3[s, d - 1]
        first_image.append(total)

    lane = lax.broadcasted_iota(jnp.int32, (ROWS, 128), 1)
    low = lane < 64
    lanes_in = lax.broadcasted_iota(jnp.int32, (72, 256), 1) < W
    row_of_8 = lax.broadcasted_iota(jnp.int32, (ROWS, 256), 0)
    bias_rows = jnp.where(lax.rem(row_of_8, 2) == 0, bias_second_ref[0:1, 0:1], bias_second_ref[0:1, 1:2])
    image = first_image
    for turn in range(ITERS):
        damped = []
        products = []
        for s in range(2):
            v = image[s]
            va, vb, vc = v[None, :, 0:128], v[None, :, 128:256], v[:, 256:384]
            turned_c = pltpu.roll(vc, 64, 1)
            v_re = jnp.where(low, vc, turned_c)[None]
            v_im = jnp.where(low, -turned_c, vc)[None]
            ma, mb, mc = gathered_f[s, :, :, 0:128], gathered_f[s, :, :, 128:256], gathered_f[s, :, :, 256:384]
            ms = gathered_swap[s]
            pieces = [ma * va - mb * vb, ma * vb + mb * va, mc * v_re + ms * v_im]
            product = jnp.concatenate([p.reshape(n * ROWS, 128) for p in pieces], axis=1).astype(BF16)
            products.append(product)
        backs = [dot(jnp.concatenate([p, p], axis=1), spread[s]) for s, p in enumerate(products)]
        for s in range(2):
            v = image[s]
            back = backs[s].reshape(n, ROWS, 384)
            ma, mb, mc = gathered_f[s, :, :, 0:128], gathered_f[s, :, :, 128:256], gathered_f[s, :, :, 256:384]
            ms = gathered_swap[s]
            qa, qb, qc = back[:, :, 0:128], back[:, :, 128:256], back[:, :, 256:384]
            oa = jnp.sum(ma * qa + mb * qb, axis=0)
            ob = jnp.sum(ma * qb - mb * qa, axis=0)
            same = jnp.sum(mc * qc, axis=0)
            cross = jnp.sum(ms * qc, axis=0)
            oc = jnp.where(low, same + pltpu.roll(same, 64, 1), cross - pltpu.roll(cross, 64, 1))
            summed = jnp.concatenate([oa, ob, oc], axis=1)
            damped.append(v - STEP * (summed - first_image[s]))

        parts = [unpack(damped[s]) for s in range(2)]
        for side, top in enumerate((ROWS - 2, 0)):
            for s in range(2):
                for q in range(2):
                    for t in range(2):
                        for h in range(2):
                            row = 8 * t + 4 * h + 2 * s + q
                            strip_rows[side, row:row + 1, :] = parts[s][q][t][top + h:top + h + 1]
            strip_out[turn, side] = strip_rows[side].astype(BF16)
        strips = []
        for i, (dc, ds) in enumerate(STRIPS):
            peer = (lax.rem(coil + dc + n, n), lax.rem(sect + ds + sections, sections))
            copy = pltpu.make_async_remote_copy(
                src_ref=strip_out.at[turn, 0 if dc > 0 else 1], dst_ref=strip_in.at[turn, i],
                send_sem=strip_send.at[turn, i], recv_sem=strip_recv.at[turn, i],
                device_id=peer, device_id_type=MESH,
            )
            if ds == 0 and i == 4:
                edge_out[turn] = jnp.concatenate(damped, axis=0).astype(BF16)
                sides = []
                for k, step in enumerate((1, -1)):
                    across = pltpu.make_async_remote_copy(
                        src_ref=edge_out.at[turn], dst_ref=edge_in.at[turn, k],
                        send_sem=edge_send.at[turn, k], recv_sem=edge_recv.at[turn, k],
                        device_id=(coil, lax.rem(sect + step + sections, sections)), device_id_type=MESH,
                    )
                    across.start()
                    sides.append(across)
            copy.start()
            strips.append(copy)

        def place_slices(values, ds):
            for s in range(2):
                for q in range(2):
                    for t in range(2):
                        grid_rows[t, pl.ds(32 + 2 * (2 + 2 * ds + s) + q, ROWS, stride=16), :] = values[s][q][t]

        def halve(first, last):
            rows = jnp.concatenate([grid_rows[0, first:last], grid_rows[1, first:last]], axis=1)
            grid_half[0, first:last] = pltpu.roll(rows, 1, 1).astype(BF16)
            grid_half[1, first:last] = rows.astype(BF16)
            grid_half[2, first:last] = pltpu.roll(rows, 255, 1).astype(BF16)

        def hidden_of(r):
            taps = jnp.concatenate([grid_half[e, 16 * r:16 * r + 48, :] for e in range(3)], axis=0)
            return jnp.maximum(dot(weight1[...], taps), 0.0).astype(BF16)

        def spots_of(r, hidden):
            spots = jnp.where(lanes_in, dot(weight2[...], hidden), 0.0)
            if r == 0:
                spots = jnp.where(coil > 0, spots, 0.0)
            if r == ROWS + 1:
                spots = jnp.where(coil < n - 1, spots, 0.0)
            return spots

        place_slices(parts, 0)
        if turn == 0:
            for copy in copies1 + copies2 + copies3:
                copy.wait_send()

            def wait_sent(d, carry):
                maps_copy(d).wait_send()
                return carry

            lax.fori_loop(1, n, wait_sent, 0)
        for k, step in enumerate((1, -1)):
            sides[k].wait_recv()
            inside = jnp.logical_and(sect - step >= 0, sect - step < sections)
            block = jnp.where(inside, edge_in[turn, k].astype(F32), 0.0)
            place_slices([unpack(block[0:ROWS]), unpack(block[ROWS:2 * ROWS])], -step)
        halve(32, 160)
        hidden = {r: hidden_of(r) for r in range(2, ROWS)}
        spots = {r: spots_of(r, hidden[r]) for r in range(2, ROWS)}

        for i, (dc, ds) in reversed(list(enumerate(STRIPS))):
            strips[i].wait_recv()
            inside = jnp.logical_and(
                jnp.logical_and(coil - dc >= 0, coil - dc < n),
                jnp.logical_and(sect - ds >= 0, sect - ds < sections),
            )
            block = jnp.where(inside, strip_in[turn, i].astype(F32), 0.0)
            for t in range(2):
                for h in range(2):
                    to = (0 if dc > 0 else 160) + 16 * h + 2 * (2 - 2 * ds)
                    grid_rows[t, to:to + 4, :] = block[8 * t + 4 * h:8 * t + 4 * h + 4]
        halve(0, 32)
        halve(160, 192)
        hidden = {r: hidden_of(r) for r in (0, 1, ROWS, ROWS + 1)}
        for r in hidden:
            spots[r] = spots_of(r, hidden[r])

        for r in range(ROWS):
            taps = spots[r][0:24] + spots[r + 1][24:48] + spots[r + 2][48:72]
            update = pltpu.roll(taps[0:8], 1, 1) + taps[8:16] + pltpu.roll(taps[16:24], 255, 1) + bias_rows
            for t in range(2):
                result[t, 4 * r:4 * r + 4, :] = update[0:4, 128 * t:128 * t + 128]
        for copy in sides + strips:
            copy.wait_send()

        image = []
        for s in range(2):
            update = [[result[t, pl.ds(2 * s + q, ROWS, stride=4), :] for t in range(2)] for q in range(2)]
            if turn < ITERS - 1:
                image.append(damped[s] + pack(*update))
            else:
                for q, value in enumerate(parts[s]):
                    for t in range(2):
                        result[t, pl.ds(2 * s + q, ROWS, stride=4), :] = value[t] + update[q][t]

    for r in range(ROWS):
        for s in range(2):
            rows = slice(4 * r + 2 * s, 4 * r + 2 * s + 2)
            out_ref[r, s, :, 0:128] = result[0, rows]
            out_ref[r, s, :, 128:W] = result[1, rows, 0:W - 128]


def per_device(n, sections, measured, coil_maps, sampling, conv_first, bias_first, conv_second, bias_second):
    height = measured.shape[0]
    by_columns = lambda t: t.transpose(1, 2, 3, 4, 0).reshape(2, 2 * W, height)
    consts = [jnp.asarray(t) for t in tables(height)]
    chips = n // 2
    x_size = min(X_CHIPS, chips // 2)
    z_size = chips // x_size
    dma = pltpu.SemaphoreType.DMA
    out = pl.pallas_call(
        lambda *refs: kernel(n, sections, *refs),
        out_shape=pltpu.VMEM((ROWS, 2, 2, W), F32),
        in_specs=[pl.BlockSpec(memory_space=pl.ANY)] * 14,
        out_specs=pl.BlockSpec(memory_space=pltpu.VMEM),
        scratch_shapes=[
            pltpu.VMEM((2, 384, height), F32),
            pltpu.VMEM((2, 384, height), F32),
            pltpu.VMEM((2, W), jnp.int32),
            pltpu.VMEM((384, 384), BF16),
            pltpu.VMEM((384, 384), BF16),
            pltpu.VMEM((height, 2 * height), BF16),
            pltpu.VMEM((height, 2 * height), BF16),
            pltpu.VMEM((54, CH), BF16),
            pltpu.VMEM((1, CH), F32),
            pltpu.VMEM((54, CH), BF16),
            pltpu.VMEM((1, 2), F32),
            pltpu.VMEM((4, 54, 144), BF16),
            pltpu.VMEM((4, 72, 54), BF16),
            pltpu.VMEM((CH, 256), BF16),
            pltpu.VMEM((2, 384, 1152), BF16),
            pltpu.VMEM((2, 768, 384), BF16),
            pltpu.VMEM((n, 2 * ROWS, 384), BF16),
            pltpu.VMEM((n, 2 * ROWS, 384), BF16),
            pltpu.VMEM((2, n, ROWS, 384), F32),
            pltpu.VMEM((2, n, ROWS, 128), F32),
            pltpu.VMEM((2, chips, 2, ROWS, 384), F32),
            pltpu.VMEM((2, chips, ROWS, 384), F32),
            pltpu.VMEM((2, z_size, x_size, ROWS, 384), F32),
            pltpu.VMEM((2, x_size - 1, z_size, ROWS, 384), F32),
            pltpu.VMEM((2, z_size, ROWS, 384), F32),
            pltpu.VMEM((2, z_size - 1, ROWS, 384), F32),
            pltpu.VMEM((256, 144), BF16),
            pltpu.VMEM((72, 256), BF16),
            pltpu.VMEM((ITERS, 2 * ROWS, 384), BF16),
            pltpu.VMEM((ITERS, 2, 2 * ROWS, 384), BF16),
            pltpu.VMEM((2, 16, 128), F32),
            pltpu.VMEM((ITERS, 2, 16, 128), BF16),
            pltpu.VMEM((ITERS, 6, 16, 128), BF16),
            pltpu.VMEM((2, 192, 128), F32),
            pltpu.VMEM((3, 192, 256), BF16),
            pltpu.VMEM((2, 4 * ROWS, 128), F32),
            dma((14,)),
            dma((n,)),
            dma((n,)),
            dma((2,)),
            dma((2,)),
            dma((2, x_size - 1)),
            dma((2, x_size - 1)),
            dma((2, z_size - 1)),
            dma((2, z_size - 1)),
            dma((ITERS, 2)),
            dma((ITERS, 2)),
            dma((ITERS, 6)),
            dma((ITERS, 6)),
        ],
        compiler_params=pltpu.CompilerParams(
            collective_id=0, has_side_effects=True, vmem_limit_bytes=60 * 1024 * 1024
        ),
        name="reconstruct",
    )(
        by_columns(measured), by_columns(coil_maps), sampling, *consts[:4],
        conv_first.T, bias_first.reshape(1, CH), conv_second, bias_second.reshape(1, 2), *consts[4:],
    )
    return out


def solution(mesh):
    n, sections = mesh.shape["coil"], mesh.shape["sect"]
    split = P(None, "coil", "sect", None, None)
    return jax.shard_map(
        lambda *args: per_device(n, sections, *args),
        mesh=mesh,
        in_specs=(split, split, P("sect", None), P(), P(), P(), P()),
        out_specs=P("coil", "sect", None, None),
        check_vma=False,
    )
```

```python
import math

import jax
import jax.numpy as jnp
import ml_dtypes
import numpy as np
from jax import lax
from jax.experimental import pallas as pl
from jax.experimental.pallas import tpu as pltpu
from jax.sharding import PartitionSpec as P

ITERS = 2
STEP = 0.5
X_CHIPS = 4
W = 192
CH = 64
BIAS_TAP = 48 + 16 + 12
ROWS = 8
F32 = jnp.float32
BF16 = jnp.bfloat16
MESH = pl.DeviceIdType.MESH

PACKED = np.concatenate([np.arange(0, 128), np.arange(192, 320), np.arange(128, 192), np.arange(320, 384)])
STRIPS = [(1, 1), (1, -1), (-1, 1), (-1, -1), (1, 0), (-1, 0)]


def split_halves(table):
    high = table.astype(ml_dtypes.bfloat16)
    low = (table - high.astype(np.float64)).astype(ml_dtypes.bfloat16)
    return high, low


def dft(length):
    index = np.arange(length)
    angle = (index[:, None] * index[None, :] % length) * (2.0 * math.pi / length)
    return np.cos(angle) / math.sqrt(length), np.sin(angle) / math.sqrt(length)


def tables(height):
    cosine, sine = dft(W)
    column = np.block([[cosine, -sine], [sine, cosine]])[PACKED][:, PACKED]
    cosine, sine = dft(height)
    row = np.concatenate([cosine, sine], axis=1)
    pick_first = np.zeros((4, 54, 144), np.float32)
    pick_second = np.zeros((4, 72, 54), np.float32)
    for a in range(3):
        for b in range(3):
            for e in range(3):
                for q in range(2):
                    tap = 2 * (9 * a + 3 * b + e) + q
                    for s in range(4):
                        pick_first[s, tap, 48 * e + 16 * a + 2 * (s + b) + q] = 1.0
                        if 0 <= s - b < 2:
                            pick_second[s, 24 * a + 8 * e + 2 * (s - b) + q, tap] = 1.0
    repeat = np.tile(np.eye(CH, dtype=np.float32), (1, 4))
    as_half = lambda t: t.astype(ml_dtypes.bfloat16)
    return split_halves(column) + split_halves(row) + (as_half(pick_first), as_half(pick_second), as_half(repeat))


def dot(a, b, dims=((1,), (0,))):
    return lax.dot_general(a, b, (dims, ((), ())), preferred_element_type=F32)


def halves(value):
    high = value.astype(BF16)
    return high, (value - high.astype(F32)).astype(BF16)


def pack_rows(value):
    return jnp.concatenate([value[0:128], value[192:320], value[128:192], value[320:384]], axis=0)


def low_lanes(shape):
    return lax.broadcasted_iota(jnp.int32, shape, len(shape) - 1) < 64


def unpack(value):
    third = value[:, 256:384]
    low = low_lanes(third.shape)
    real = (value[:, 0:128], jnp.where(low, third, 0.0))
    imag = (value[:, 128:256], jnp.where(low, pltpu.roll(third, 64, 1), 0.0))
    return real, imag


def pack(real, imag):
    third = jnp.where(low_lanes(real[1].shape), real[1], pltpu.roll(imag[1], 64, 1))
    return jnp.concatenate([real[0], imag[0], third], axis=1)


def kernel(n, sections, meas_hbm, maps_hbm, samp_hbm, th_hbm, tl_hbm, eh_hbm, el_hbm,
           first_hbm, bias_first_hbm, second_hbm, bias_second_hbm, pick_first_hbm, pick_second_hbm, repeat_hbm, out_ref,
           meas, maps, samp_ref, th, tl, eh, el,
           first_ref, bias_first_ref, second_ref, bias_second_ref, pick_first_ref, pick_second_ref, repeat_ref, masked, spread, outgoing, gathered, gathered_f, gathered_swap,
           part, got1, sum1, got2, sum2, got3, weight1, weight2, edge_out, edge_in, strip_rows, strip_out, strip_in, grid_rows, grid_half,
           result, load_sem, maps_send, maps_recv, rs1_send, rs1_recv, rs2_send, rs2_recv, rs3_send, rs3_recv,
           edge_send, edge_recv,
           strip_send, strip_recv):
    coil = lax.axis_index("coil")
    sect = lax.axis_index("sect")
    core = lax.rem(coil, 2)
    x_size = sum1.shape[2]
    z_size = sum1.shape[1]
    plane = 2 * x_size
    spot_in_plane = lax.rem(coil, plane)
    x = lax.rem(coil // 2, x_size)
    z = coil // plane

    loads = [
        pltpu.make_async_copy(src, dst, load_sem.at[i])
        for i, (src, dst) in enumerate(
            [
                (samp_hbm, samp_ref), (th_hbm, th), (tl_hbm, tl), (meas_hbm, meas), (eh_hbm, eh), (el_hbm, el),
                (maps_hbm, maps), (first_hbm, first_ref), (bias_first_hbm, bias_first_ref), (second_hbm, second_ref),
                (bias_second_hbm, bias_second_ref), (pick_first_hbm, pick_first_ref),
                (pick_second_hbm, pick_second_ref), (repeat_hbm, repeat_ref),
            ]
        )
    ]
    for load in loads[:7]:
        load.start()

    barrier = pltpu.get_barrier_semaphore()

    def greet(d, carry):
        pl.semaphore_signal(barrier, inc=1, device_id=(lax.rem(coil + d, n), sect), device_id_type=MESH)
        return carry

    lax.fori_loop(1, n, greet, 0)
    for dc in (-1, 0, 1):
        for ds in (-1, 1):
            peer = (lax.rem(coil + dc + n, n), lax.rem(sect + ds + sections, sections))
            pl.semaphore_signal(barrier, inc=1, device_id=peer, device_id_type=MESH)

    for load in loads[7:]:
        load.start()
    for load in loads[:3]:
        load.wait()
    flags = jnp.concatenate([samp_ref[...].astype(F32), jnp.zeros((2, 64), F32)], axis=1)
    flags = jnp.concatenate([flags, jnp.zeros((6, 256), F32)], axis=0).T
    table = jnp.concatenate([th[...], tl[...], th[...]], axis=1)

    for load in loads[3:7]:
        load.wait()
    copies1 = []
    columns = []
    for s in range(2):
        flag = flags[:, s:s + 1]
        flag = jnp.concatenate([flag[0:128], flag[0:128], flag[128:W], flag[128:W]], axis=0)
        xh, xl = halves(pack_rows(meas[s]) * flag)
        columns.append(dot(table, jnp.concatenate([xh, xh, xl], axis=0)))
    planes = []
    for s in range(2):
        zh, zl = halves(columns[s])
        planes.append(dot(jnp.concatenate([zh, zl, zh], axis=1), jnp.concatenate([eh[...], eh[...], el[...]], axis=0)))
    for s in range(2):
        both = planes[s]
        height = both.shape[1] // 2
        by_cos, by_sin = both[:, :height], both[:, height:]
        m = pack_rows(maps[s])
        terms = []
        for r0, i0, size in ((0, 128, 128), (256, 320, 64)):
            re, im = slice(r0, r0 + size), slice(i0, i0 + size)
            y_re = by_cos[re] - by_sin[im]
            y_im = by_cos[im] + by_sin[re]
            terms += [m[re] * y_re + m[im] * y_im, m[re] * y_im - m[im] * y_re]
        part[s] = jnp.concatenate(terms, axis=0).T.reshape(n // 2, 2, ROWS, 384)
        if s == 0:
            pl.semaphore_wait(barrier, n - 1 + 6)
        copy = pltpu.make_async_remote_copy(
            src_ref=part.at[s, :, 1 - core], dst_ref=got1.at[s], send_sem=rs1_send.at[s], recv_sem=rs1_recv.at[s],
            device_id=(coil + 1 - 2 * core, sect), device_id_type=MESH,
        )
        copy.start()
        copies1.append(copy)

    turned = [pack_rows(maps[s]).T.reshape(n, ROWS, 384) for s in range(2)]
    outgoing[...] = jnp.concatenate(turned, axis=1).astype(BF16)
    gathered[coil] = outgoing[coil]

    def maps_copy(d):
        peer = lax.rem(z + d // plane, z_size) * plane + lax.rem(spot_in_plane + d, plane)
        return pltpu.make_async_remote_copy(
            src_ref=outgoing.at[peer], dst_ref=gathered.at[coil], send_sem=maps_send.at[d], recv_sem=maps_recv.at[d],
            device_id=(peer, sect), device_id_type=MESH,
        )

    def send_maps(d, carry):
        maps_copy(d).start()
        return carry

    lax.fori_loop(plane, n, send_maps, 0)

    copies2 = []
    for s in range(2):
        copies1[s].wait_recv()
        sum1[s] = (part[s, :, core] + got1[s]).reshape(z_size, x_size, ROWS, 384)
        for d in range(1, x_size):
            to = lax.rem(x + d, x_size)
            copy = pltpu.make_async_remote_copy(
                src_ref=sum1.at[s, :, to], dst_ref=got2.at[s, d - 1],
                send_sem=rs2_send.at[s, d - 1], recv_sem=rs2_recv.at[s, d - 1],
                device_id=((z * x_size + to) * 2 + core, sect), device_id_type=MESH,
            )
            copy.start()
            copies2.append(copy)

    lax.fori_loop(1, plane, send_maps, 0)
    for s in range(2):
        mask = samp_ref[s:s + 1, :].astype(F32)
        mask = jnp.concatenate([mask, jnp.zeros((1, 64), F32)], axis=1)
        tail = mask[:, 128:256]
        mask = jnp.concatenate([mask[:, 0:128], mask[:, 0:128], tail + pltpu.roll(tail, 64, 1)], axis=1)
        high = (th[...].astype(F32) * mask).astype(BF16)
        masked[s, :, 0:384] = high
        masked[s, :, 384:768] = (tl[...].astype(F32) * mask).astype(BF16)
        masked[s, :, 768:1152] = high
    for s in range(2):
        last = ((1,), (1,))
        mh, ml = masked[s, :, 0:384], masked[s, :, 384:768]
        high, low = halves(dot(masked[s], jnp.concatenate([mh, mh, ml], axis=1), last))
        spread[s, 0:384] = high
        spread[s, 384:768] = low

    copies3 = []
    for s in range(2):
        total = sum1[s, :, x]
        for d in range(1, x_size):
            copies2[s * (x_size - 1) + d - 1].wait_recv()
            total = total + got2[s, d - 1]
        sum2[s] = total
        for d in range(1, z_size):
            to = lax.rem(z + d, z_size)
            copy = pltpu.make_async_remote_copy(
                src_ref=sum2.at[s, to], dst_ref=got3.at[s, d - 1],
                send_sem=rs3_send.at[s, d - 1], recv_sem=rs3_recv.at[s, d - 1],
                device_id=((to * x_size + x) * 2 + core, sect), device_id_type=MESH,
            )
            copy.start()
            copies3.append(copy)

    for load in loads[7:]:
        load.wait()
    repeated = dot(second_ref[...], repeat_ref[...]).astype(BF16)
    of_slice = lax.broadcasted_iota(jnp.int32, (72, 256), 1) // 64
    second = jnp.zeros((72, 256), F32)
    for s in range(4):
        inside = jnp.logical_and(2 * sect - 1 + s >= 0, 2 * sect - 1 + s < 2 * sections)
        block = dot(pick_second_ref[s], repeated)
        second = second + jnp.where(jnp.logical_and(of_slice == s, inside), block, 0.0)
    weight2[...] = second.astype(BF16)
    diagonal = lax.broadcasted_iota(jnp.int32, (64, 64), 0) == lax.broadcasted_iota(jnp.int32, (64, 64), 1)
    bias_column = jnp.sum(jnp.where(diagonal, bias_first_ref[...], 0.0), axis=1, keepdims=True)
    bias_high = bias_column.astype(BF16).astype(F32)
    bias_rest = bias_column - bias_high
    bias_middle = bias_rest.astype(BF16).astype(F32)
    spot = lax.broadcasted_iota(jnp.int32, (64, 144), 1)
    bias_taps = jnp.where(spot == BIAS_TAP, bias_high, 0.0)
    bias_taps = jnp.where(spot == BIAS_TAP + 1, bias_middle, bias_taps)
    bias_taps = jnp.where(spot == BIAS_TAP + 2, bias_rest - bias_middle, bias_taps)
    for s in range(4):
        block = dot(first_ref[...], pick_first_ref[s], ((0,), (0,)))
        weight1[64 * s:64 * s + 64] = (block + bias_taps).astype(BF16)
    place = lax.rem(lax.broadcasted_iota(jnp.int32, (192, 128), 0), 16)
    for t in range(2):
        grid_rows[t] = jnp.where(jnp.logical_and(place >= 12, place < 15), 1.0, 0.0)

    def wait_maps(d, carry):
        maps_copy(d).wait_recv()
        return carry

    lax.fori_loop(1, n, wait_maps, 0)
    every = gathered[...].astype(F32)
    for s in range(2):
        mine = every[:, ROWS * s:ROWS * s + ROWS, :]
        gathered_f[s] = mine
        gathered_swap[s] = pltpu.roll(mine[:, :, 256:384].reshape(n * ROWS, 128), 64, 1).reshape(n, ROWS, 128)

    first_image = []
    for s in range(2):
        total = sum2[s, z]
        for d in range(1, z_size):
            copies3[s * (z_size - 1) + d - 1].wait_recv()
            total = total + got3[s, d - 1]
        first_image.append(total)

    lane = lax.broadcasted_iota(jnp.int32, (ROWS, 128), 1)
    low = lane < 64
    lanes_in = lax.broadcasted_iota(jnp.int32, (72, 256), 1) < W
    row_of_8 = lax.broadcasted_iota(jnp.int32, (ROWS, 256), 0)
    bias_rows = jnp.where(lax.rem(row_of_8, 2) == 0, bias_second_ref[0:1, 0:1], bias_second_ref[0:1, 1:2])
    image = first_image
    for turn in range(ITERS):
        damped = []
        products = []
        for s in range(2):
            v = image[s]
            va, vb, vc = v[None, :, 0:128], v[None, :, 128:256], v[:, 256:384]
            turned_c = pltpu.roll(vc, 64, 1)
            v_re = jnp.where(low, vc, turned_c)[None]
            v_im = jnp.where(low, -turned_c, vc)[None]
            ma, mb, mc = gathered_f[s, :, :, 0:128], gathered_f[s, :, :, 128:256], gathered_f[s, :, :, 256:384]
            ms = gathered_swap[s]
            pieces = [ma * va - mb * vb, ma * vb + mb * va, mc * v_re + ms * v_im]
            product = jnp.concatenate([p.reshape(n * ROWS, 128) for p in pieces], axis=1).astype(BF16)
            products.append(product)
        backs = [dot(jnp.concatenate([p, p], axis=1), spread[s]) for s, p in enumerate(products)]
        for s in range(2):
            v = image[s]
            back = backs[s].reshape(n, ROWS, 384)
            ma, mb, mc = gathered_f[s, :, :, 0:128], gathered_f[s, :, :, 128:256], gathered_f[s, :, :, 256:384]
            ms = gathered_swap[s]
            qa, qb, qc = back[:, :, 0:128], back[:, :, 128:256], back[:, :, 256:384]
            oa = jnp.sum(ma * qa + mb * qb, axis=0)
            ob = jnp.sum(ma * qb - mb * qa, axis=0)
            same = jnp.sum(mc * qc, axis=0)
            cross = jnp.sum(ms * qc, axis=0)
            oc = jnp.where(low, same + pltpu.roll(same, 64, 1), cross - pltpu.roll(cross, 64, 1))
            summed = jnp.concatenate([oa, ob, oc], axis=1)
            damped.append(v - STEP * (summed - first_image[s]))

        parts = [unpack(damped[s]) for s in range(2)]
        for side, top in enumerate((ROWS - 2, 0)):
            for s in range(2):
                for q in range(2):
                    for t in range(2):
                        for h in range(2):
                            row = 8 * t + 4 * h + 2 * s + q
                            strip_rows[side, row:row + 1, :] = parts[s][q][t][top + h:top + h + 1]
            strip_out[turn, side] = strip_rows[side].astype(BF16)
        strips = []
        for i, (dc, ds) in enumerate(STRIPS):
            peer = (lax.rem(coil + dc + n, n), lax.rem(sect + ds + sections, sections))
            copy = pltpu.make_async_remote_copy(
                src_ref=strip_out.at[turn, 0 if dc > 0 else 1], dst_ref=strip_in.at[turn, i],
                send_sem=strip_send.at[turn, i], recv_sem=strip_recv.at[turn, i],
                device_id=peer, device_id_type=MESH,
            )
            if ds == 0 and i == 4:
                edge_out[turn] = jnp.concatenate(damped, axis=0).astype(BF16)
                sides = []
                for k, step in enumerate((1, -1)):
                    across = pltpu.make_async_remote_copy(
                        src_ref=edge_out.at[turn], dst_ref=edge_in.at[turn, k],
                        send_sem=edge_send.at[turn, k], recv_sem=edge_recv.at[turn, k],
                        device_id=(coil, lax.rem(sect + step + sections, sections)), device_id_type=MESH,
                    )
                    across.start()
                    sides.append(across)
            copy.start()
            strips.append(copy)

        def place_slices(values, ds):
            for s in range(2):
                for q in range(2):
                    for t in range(2):
                        grid_rows[t, pl.ds(32 + 2 * (2 + 2 * ds + s) + q, ROWS, stride=16), :] = values[s][q][t]

        def halve(first, last):
            rows = jnp.concatenate([grid_rows[0, first:last], grid_rows[1, first:last]], axis=1)
            grid_half[0, first:last] = pltpu.roll(rows, 1, 1).astype(BF16)
            grid_half[1, first:last] = rows.astype(BF16)
            grid_half[2, first:last] = pltpu.roll(rows, 255, 1).astype(BF16)

        def hidden_of(r):
            taps = jnp.concatenate([grid_half[e, 16 * r:16 * r + 48, :] for e in range(3)], axis=0)
            return jnp.maximum(dot(weight1[...], taps), 0.0).astype(BF16)

        def spots_of(r, hidden):
            spots = jnp.where(lanes_in, dot(weight2[...], hidden), 0.0)
            if r == 0:
                spots = jnp.where(coil > 0, spots, 0.0)
            if r == ROWS + 1:
                spots = jnp.where(coil < n - 1, spots, 0.0)
            return spots

        place_slices(parts, 0)
        if turn == 0:
            for copy in copies1 + copies2 + copies3:
                copy.wait_send()

            def wait_sent(d, carry):
                maps_copy(d).wait_send()
                return carry

            lax.fori_loop(1, n, wait_sent, 0)
        for k, step in enumerate((1, -1)):
            sides[k].wait_recv()
            inside = jnp.logical_and(sect - step >= 0, sect - step < sections)
            block = jnp.where(inside, edge_in[turn, k].astype(F32), 0.0)
            place_slices([unpack(block[0:ROWS]), unpack(block[ROWS:2 * ROWS])], -step)
        halve(32, 160)
        hidden = {r: hidden_of(r) for r in range(2, ROWS)}
        spots = {r: spots_of(r, hidden[r]) for r in range(2, ROWS)}

        for i, (dc, ds) in reversed(list(enumerate(STRIPS))):
            strips[i].wait_recv()
            inside = jnp.logical_and(
                jnp.logical_and(coil - dc >= 0, coil - dc < n),
                jnp.logical_and(sect - ds >= 0, sect - ds < sections),
            )
            block = jnp.where(inside, strip_in[turn, i].astype(F32), 0.0)
            for t in range(2):
                for h in range(2):
                    to = (0 if dc > 0 else 160) + 16 * h + 2 * (2 - 2 * ds)
                    grid_rows[t, to:to + 4, :] = block[8 * t + 4 * h:8 * t + 4 * h + 4]
        halve(0, 32)
        halve(160, 192)
        hidden = {r: hidden_of(r) for r in (0, 1, ROWS, ROWS + 1)}
        for r in hidden:
            spots[r] = spots_of(r, hidden[r])

        for r in range(ROWS):
            taps = spots[r][0:24] + spots[r + 1][24:48] + spots[r + 2][48:72]
            update = pltpu.roll(taps[0:8], 1, 1) + taps[8:16] + pltpu.roll(taps[16:24], 255, 1) + bias_rows
            for t in range(2):
                result[t, 4 * r:4 * r + 4, :] = update[0:4, 128 * t:128 * t + 128]
        for copy in sides + strips:
            copy.wait_send()

        image = []
        for s in range(2):
            update = [[result[t, pl.ds(2 * s + q, ROWS, stride=4), :] for t in range(2)] for q in range(2)]
            if turn < ITERS - 1:
                image.append(damped[s] + pack(*update))
            else:
                for q, value in enumerate(parts[s]):
                    for t in range(2):
                        result[t, pl.ds(2 * s + q, ROWS, stride=4), :] = value[t] + update[q][t]

    for r in range(ROWS):
        for s in range(2):
            rows = slice(4 * r + 2 * s, 4 * r + 2 * s + 2)
            out_ref[r, s, :, 0:128] = result[0, rows]
            out_ref[r, s, :, 128:W] = result[1, rows, 0:W - 128]


def per_device(n, sections, measured, coil_maps, sampling, conv_first, bias_first, conv_second, bias_second):
    height = measured.shape[0]
    by_columns = lambda t: t.transpose(1, 2, 3, 4, 0).reshape(2, 2 * W, height)
    consts = [jnp.asarray(t) for t in tables(height)]
    chips = n // 2
    x_size = min(X_CHIPS, chips // 2)
    z_size = chips // x_size
    dma = pltpu.SemaphoreType.DMA
    out = pl.pallas_call(
        lambda *refs: kernel(n, sections, *refs),
        out_shape=pltpu.VMEM((ROWS, 2, 2, W), F32),
        in_specs=[pl.BlockSpec(memory_space=pl.ANY)] * 14,
        out_specs=pl.BlockSpec(memory_space=pltpu.VMEM),
        scratch_shapes=[
            pltpu.VMEM((2, 384, height), F32),
            pltpu.VMEM((2, 384, height), F32),
            pltpu.VMEM((2, W), jnp.int32),
            pltpu.VMEM((384, 384), BF16),
            pltpu.VMEM((384, 384), BF16),
            pltpu.VMEM((height, 2 * height), BF16),
            pltpu.VMEM((height, 2 * height), BF16),
            pltpu.VMEM((54, CH), BF16),
            pltpu.VMEM((1, CH), F32),
            pltpu.VMEM((54, CH), BF16),
            pltpu.VMEM((1, 2), F32),
            pltpu.VMEM((4, 54, 144), BF16),
            pltpu.VMEM((4, 72, 54), BF16),
            pltpu.VMEM((CH, 256), BF16),
            pltpu.VMEM((2, 384, 1152), BF16),
            pltpu.VMEM((2, 768, 384), BF16),
            pltpu.VMEM((n, 2 * ROWS, 384), BF16),
            pltpu.VMEM((n, 2 * ROWS, 384), BF16),
            pltpu.VMEM((2, n, ROWS, 384), F32),
            pltpu.VMEM((2, n, ROWS, 128), F32),
            pltpu.VMEM((2, chips, 2, ROWS, 384), F32),
            pltpu.VMEM((2, chips, ROWS, 384), F32),
            pltpu.VMEM((2, z_size, x_size, ROWS, 384), F32),
            pltpu.VMEM((2, x_size - 1, z_size, ROWS, 384), F32),
            pltpu.VMEM((2, z_size, ROWS, 384), F32),
            pltpu.VMEM((2, z_size - 1, ROWS, 384), F32),
            pltpu.VMEM((256, 144), BF16),
            pltpu.VMEM((72, 256), BF16),
            pltpu.VMEM((ITERS, 2 * ROWS, 384), BF16),
            pltpu.VMEM((ITERS, 2, 2 * ROWS, 384), BF16),
            pltpu.VMEM((2, 16, 128), F32),
            pltpu.VMEM((ITERS, 2, 16, 128), BF16),
            pltpu.VMEM((ITERS, 6, 16, 128), BF16),
            pltpu.VMEM((2, 192, 128), F32),
            pltpu.VMEM((3, 192, 256), BF16),
            pltpu.VMEM((2, 4 * ROWS, 128), F32),
            dma((14,)),
            dma((n,)),
            dma((n,)),
            dma((2,)),
            dma((2,)),
            dma((2, x_size - 1)),
            dma((2, x_size - 1)),
            dma((2, z_size - 1)),
            dma((2, z_size - 1)),
            dma((ITERS, 2)),
            dma((ITERS, 2)),
            dma((ITERS, 6)),
            dma((ITERS, 6)),
        ],
        compiler_params=pltpu.CompilerParams(
            collective_id=0, has_side_effects=True, vmem_limit_bytes=60 * 1024 * 1024
        ),
        name="reconstruct",
    )(
        by_columns(measured), by_columns(coil_maps), sampling, *consts[:4],
        conv_first.T, bias_first.reshape(1, CH), conv_second, bias_second.reshape(1, 2), *consts[4:],
    )
    return out


def solution(mesh):
    n, sections = mesh.shape["coil"], mesh.shape["sect"]
    split = P(None, "coil", "sect", None, None)
    return jax.shard_map(
        lambda *args: per_device(n, sections, *args),
        mesh=mesh,
        in_specs=(split, split, P("sect", None), P(), P(), P(), P()),
        out_specs=P("coil", "sect", None, None),
        check_vma=False,
    )
```

```python
import math

import jax
import jax.numpy as jnp
import ml_dtypes
import numpy as np
from jax import lax
from jax.experimental import pallas as pl
from jax.experimental.pallas import tpu as pltpu
from jax.sharding import PartitionSpec as P

ITERS = 2
STEP = 0.5
X_CHIPS = 4
W = 192
CH = 64
BIAS_TAP = 48 + 16 + 12
ROWS = 8
F32 = jnp.float32
BF16 = jnp.bfloat16
MESH = pl.DeviceIdType.MESH

PACKED = np.concatenate([np.arange(0, 128), np.arange(192, 320), np.arange(128, 192), np.arange(320, 384)])
STRIPS = [(1, 1), (1, -1), (-1, 1), (-1, -1), (1, 0), (-1, 0)]


def split_halves(table):
    high = table.astype(ml_dtypes.bfloat16)
    low = (table - high.astype(np.float64)).astype(ml_dtypes.bfloat16)
    return high, low


def dft(length):
    index = np.arange(length)
    angle = (index[:, None] * index[None, :] % length) * (2.0 * math.pi / length)
    return np.cos(angle) / math.sqrt(length), np.sin(angle) / math.sqrt(length)


def tables(height):
    cosine, sine = dft(W)
    column = np.block([[cosine, -sine], [sine, cosine]])[PACKED][:, PACKED]
    cosine, sine = dft(height)
    row = np.concatenate([cosine, sine], axis=1)
    pick_first = np.zeros((4, 54, 144), np.float32)
    pick_second = np.zeros((4, 72, 54), np.float32)
    for a in range(3):
        for b in range(3):
            for e in range(3):
                for q in range(2):
                    tap = 2 * (9 * a + 3 * b + e) + q
                    for s in range(4):
                        pick_first[s, tap, 48 * e + 16 * a + 2 * (s + b) + q] = 1.0
                        if 0 <= s - b < 2:
                            pick_second[s, 24 * a + 8 * e + 2 * (s - b) + q, tap] = 1.0
    repeat = np.tile(np.eye(CH, dtype=np.float32), (1, 4))
    as_half = lambda t: t.astype(ml_dtypes.bfloat16)
    return split_halves(column) + split_halves(row) + (as_half(pick_first), as_half(pick_second), as_half(repeat))


def dot(a, b, dims=((1,), (0,))):
    return lax.dot_general(a, b, (dims, ((), ())), preferred_element_type=F32)


def halves(value):
    high = value.astype(BF16)
    return high, (value - high.astype(F32)).astype(BF16)


def pack_rows(value):
    return jnp.concatenate([value[0:128], value[192:320], value[128:192], value[320:384]], axis=0)


def low_lanes(shape):
    return lax.broadcasted_iota(jnp.int32, shape, len(shape) - 1) < 64


def unpack(value):
    third = value[:, 256:384]
    low = low_lanes(third.shape)
    real = (value[:, 0:128], jnp.where(low, third, 0.0))
    imag = (value[:, 128:256], jnp.where(low, pltpu.roll(third, 64, 1), 0.0))
    return real, imag


def pack(real, imag):
    third = jnp.where(low_lanes(real[1].shape), real[1], pltpu.roll(imag[1], 64, 1))
    return jnp.concatenate([real[0], imag[0], third], axis=1)


def kernel(n, sections, meas_hbm, maps_hbm, samp_hbm, th_hbm, tl_hbm, eh_hbm, el_hbm,
           first_hbm, bias_first_hbm, second_hbm, bias_second_hbm, pick_first_hbm, pick_second_hbm, repeat_hbm, out_ref,
           meas, maps, samp_ref, th, tl, eh, el,
           first_ref, bias_first_ref, second_ref, bias_second_ref, pick_first_ref, pick_second_ref, repeat_ref, masked, spread, outgoing, gathered, gathered_f, gathered_swap,
           part, got1, sum1, got2, sum2, got3, weight1, weight2, edge_out, edge_in, strip_rows, strip_out, strip_in, grid_rows, grid_half,
           result, load_sem, maps_send, maps_recv, rs1_send, rs1_recv, rs2_send, rs2_recv, rs3_send, rs3_recv,
           edge_send, edge_recv,
           strip_send, strip_recv):
    coil = lax.axis_index("coil")
    sect = lax.axis_index("sect")
    core = lax.rem(coil, 2)
    x_size = sum1.shape[2]
    z_size = sum1.shape[1]
    plane = 2 * x_size
    spot_in_plane = lax.rem(coil, plane)
    x = lax.rem(coil // 2, x_size)
    z = coil // plane

    loads = [
        pltpu.make_async_copy(src, dst, load_sem.at[i])
        for i, (src, dst) in enumerate(
            [
                (samp_hbm, samp_ref), (th_hbm, th), (tl_hbm, tl), (meas_hbm, meas), (eh_hbm, eh), (el_hbm, el),
                (maps_hbm, maps), (first_hbm, first_ref), (bias_first_hbm, bias_first_ref), (second_hbm, second_ref),
                (bias_second_hbm, bias_second_ref), (pick_first_hbm, pick_first_ref),
                (pick_second_hbm, pick_second_ref), (repeat_hbm, repeat_ref),
            ]
        )
    ]
    for load in loads[:7]:
        load.start()

    barrier = pltpu.get_barrier_semaphore()

    def greet(d, carry):
        pl.semaphore_signal(barrier, inc=1, device_id=(lax.rem(coil + d, n), sect), device_id_type=MESH)
        return carry

    lax.fori_loop(1, n, greet, 0)
    for dc in (-1, 0, 1):
        for ds in (-1, 1):
            peer = (lax.rem(coil + dc + n, n), lax.rem(sect + ds + sections, sections))
            pl.semaphore_signal(barrier, inc=1, device_id=peer, device_id_type=MESH)

    for load in loads[7:]:
        load.start()
    for load in loads[:3]:
        load.wait()
    flags = jnp.concatenate([samp_ref[...].astype(F32), jnp.zeros((2, 64), F32)], axis=1)
    flags = jnp.concatenate([flags, jnp.zeros((6, 256), F32)], axis=0).T
    table = jnp.concatenate([th[...], tl[...], th[...]], axis=1)

    for load in loads[3:7]:
        load.wait()
    copies1 = []
    columns = []
    for s in range(2):
        flag = flags[:, s:s + 1]
        flag = jnp.concatenate([flag[0:128], flag[0:128], flag[128:W], flag[128:W]], axis=0)
        xh, xl = halves(pack_rows(meas[s]) * flag)
        columns.append(dot(table, jnp.concatenate([xh, xh, xl], axis=0)))
    planes = []
    for s in range(2):
        zh, zl = halves(columns[s])
        planes.append(dot(jnp.concatenate([zh, zl, zh], axis=1), jnp.concatenate([eh[...], eh[...], el[...]], axis=0)))
    for s in range(2):
        both = planes[s]
        height = both.shape[1] // 2
        by_cos, by_sin = both[:, :height], both[:, height:]
        m = pack_rows(maps[s])
        terms = []
        for r0, i0, size in ((0, 128, 128), (256, 320, 64)):
            re, im = slice(r0, r0 + size), slice(i0, i0 + size)
            y_re = by_cos[re] - by_sin[im]
            y_im = by_cos[im] + by_sin[re]
            terms += [m[re] * y_re + m[im] * y_im, m[re] * y_im - m[im] * y_re]
        part[s] = jnp.concatenate(terms, axis=0).T.reshape(n // 2, 2, ROWS, 384)
        if s == 0:
            pl.semaphore_wait(barrier, n - 1 + 6)
        copy = pltpu.make_async_remote_copy(
            src_ref=part.at[s, :, 1 - core], dst_ref=got1.at[s], send_sem=rs1_send.at[s], recv_sem=rs1_recv.at[s],
            device_id=(coil + 1 - 2 * core, sect), device_id_type=MESH,
        )
        copy.start()
        copies1.append(copy)

    turned = [pack_rows(maps[s]).T.reshape(n, ROWS, 384) for s in range(2)]
    outgoing[...] = jnp.concatenate(turned, axis=1).astype(BF16)
    gathered[coil] = outgoing[coil]

    def maps_copy(d):
        peer = lax.rem(z + d // plane, z_size) * plane + lax.rem(spot_in_plane + d, plane)
        return pltpu.make_async_remote_copy(
            src_ref=outgoing.at[peer], dst_ref=gathered.at[coil], send_sem=maps_send.at[d], recv_sem=maps_recv.at[d],
            device_id=(peer, sect), device_id_type=MESH,
        )

    def send_maps(d, carry):
        maps_copy(d).start()
        return carry

    def send_far(d, carry):
        maps_copy(plane + lax.rem(d, n - plane)).start()
        return carry

    lax.fori_loop(plane, n, send_far, 0)

    copies2 = []
    for s in range(2):
        copies1[s].wait_recv()
        sum1[s] = (part[s, :, core] + got1[s]).reshape(z_size, x_size, ROWS, 384)
        for d in range(1, x_size):
            to = lax.rem(x + d, x_size)
            copy = pltpu.make_async_remote_copy(
                src_ref=sum1.at[s, :, to], dst_ref=got2.at[s, d - 1],
                send_sem=rs2_send.at[s, d - 1], recv_sem=rs2_recv.at[s, d - 1],
                device_id=((z * x_size + to) * 2 + core, sect), device_id_type=MESH,
            )
            copy.start()
            copies2.append(copy)

    lax.fori_loop(1, plane, send_maps, 0)
    for s in range(2):
        mask = samp_ref[s:s + 1, :].astype(F32)
        mask = jnp.concatenate([mask, jnp.zeros((1, 64), F32)], axis=1)
        tail = mask[:, 128:256]
        mask = jnp.concatenate([mask[:, 0:128], mask[:, 0:128], tail + pltpu.roll(tail, 64, 1)], axis=1)
        high = (th[...].astype(F32) * mask).astype(BF16)
        masked[s, :, 0:384] = high
        masked[s, :, 384:768] = (tl[...].astype(F32) * mask).astype(BF16)
        masked[s, :, 768:1152] = high
    for s in range(2):
        last = ((1,), (1,))
        mh, ml = masked[s, :, 0:384], masked[s, :, 384:768]
        high, low = halves(dot(masked[s], jnp.concatenate([mh, mh, ml], axis=1), last))
        spread[s, 0:384] = high
        spread[s, 384:768] = low

    copies3 = []
    for s in range(2):
        total = sum1[s, :, x]
        for d in range(1, x_size):
            copies2[s * (x_size - 1) + d - 1].wait_recv()
            total = total + got2[s, d - 1]
        sum2[s] = total
        for d in range(1, z_size):
            to = lax.rem(z + d, z_size)
            copy = pltpu.make_async_remote_copy(
                src_ref=sum2.at[s, to], dst_ref=got3.at[s, d - 1],
                send_sem=rs3_send.at[s, d - 1], recv_sem=rs3_recv.at[s, d - 1],
                device_id=((to * x_size + x) * 2 + core, sect), device_id_type=MESH,
            )
            copy.start()
            copies3.append(copy)

    for load in loads[7:]:
        load.wait()
    repeated = dot(second_ref[...], repeat_ref[...]).astype(BF16)
    of_slice = lax.broadcasted_iota(jnp.int32, (72, 256), 1) // 64
    second = jnp.zeros((72, 256), F32)
    for s in range(4):
        inside = jnp.logical_and(2 * sect - 1 + s >= 0, 2 * sect - 1 + s < 2 * sections)
        block = dot(pick_second_ref[s], repeated)
        second = second + jnp.where(jnp.logical_and(of_slice == s, inside), block, 0.0)
    weight2[...] = second.astype(BF16)
    diagonal = lax.broadcasted_iota(jnp.int32, (64, 64), 0) == lax.broadcasted_iota(jnp.int32, (64, 64), 1)
    bias_column = jnp.sum(jnp.where(diagonal, bias_first_ref[...], 0.0), axis=1, keepdims=True)
    bias_high = bias_column.astype(BF16).astype(F32)
    bias_rest = bias_column - bias_high
    bias_middle = bias_rest.astype(BF16).astype(F32)
    spot = lax.broadcasted_iota(jnp.int32, (64, 144), 1)
    bias_taps = jnp.where(spot == BIAS_TAP, bias_high, 0.0)
    bias_taps = jnp.where(spot == BIAS_TAP + 1, bias_middle, bias_taps)
    bias_taps = jnp.where(spot == BIAS_TAP + 2, bias_rest - bias_middle, bias_taps)
    for s in range(4):
        block = dot(first_ref[...], pick_first_ref[s], ((0,), (0,)))
        weight1[64 * s:64 * s + 64] = (block + bias_taps).astype(BF16)
    place = lax.rem(lax.broadcasted_iota(jnp.int32, (192, 128), 0), 16)
    for t in range(2):
        grid_rows[t] = jnp.where(jnp.logical_and(place >= 12, place < 15), 1.0, 0.0)

    def wait_maps(d, carry):
        maps_copy(d).wait_recv()
        return carry

    lax.fori_loop(1, n, wait_maps, 0)
    every = gathered[...].astype(F32)
    for s in range(2):
        mine = every[:, ROWS * s:ROWS * s + ROWS, :]
        gathered_f[s] = mine
        gathered_swap[s] = pltpu.roll(mine[:, :, 256:384].reshape(n * ROWS, 128), 64, 1).reshape(n, ROWS, 128)

    first_image = []
    for s in range(2):
        total = sum2[s, z]
        for d in range(1, z_size):
            copies3[s * (z_size - 1) + d - 1].wait_recv()
            total = total + got3[s, d - 1]
        first_image.append(total)

    lane = lax.broadcasted_iota(jnp.int32, (ROWS, 128), 1)
    low = lane < 64
    lanes_in = lax.broadcasted_iota(jnp.int32, (72, 256), 1) < W
    row_of_8 = lax.broadcasted_iota(jnp.int32, (ROWS, 256), 0)
    bias_rows = jnp.where(lax.rem(row_of_8, 2) == 0, bias_second_ref[0:1, 0:1], bias_second_ref[0:1, 1:2])
    image = first_image
    for turn in range(ITERS):
        damped = []
        products = []
        for s in range(2):
            v = image[s]
            va, vb, vc = v[None, :, 0:128], v[None, :, 128:256], v[:, 256:384]
            turned_c = pltpu.roll(vc, 64, 1)
            v_re = jnp.where(low, vc, turned_c)[None]
            v_im = jnp.where(low, -turned_c, vc)[None]
            ma, mb, mc = gathered_f[s, :, :, 0:128], gathered_f[s, :, :, 128:256], gathered_f[s, :, :, 256:384]
            ms = gathered_swap[s]
            pieces = [ma * va - mb * vb, ma * vb + mb * va, mc * v_re + ms * v_im]
            product = jnp.concatenate([p.reshape(n * ROWS, 128) for p in pieces], axis=1).astype(BF16)
            products.append(product)
        backs = [dot(jnp.concatenate([p, p], axis=1), spread[s]) for s, p in enumerate(products)]
        for s in range(2):
            v = image[s]
            back = backs[s].reshape(n, ROWS, 384)
            ma, mb, mc = gathered_f[s, :, :, 0:128], gathered_f[s, :, :, 128:256], gathered_f[s, :, :, 256:384]
            ms = gathered_swap[s]
            qa, qb, qc = back[:, :, 0:128], back[:, :, 128:256], back[:, :, 256:384]
            oa = jnp.sum(ma * qa + mb * qb, axis=0)
            ob = jnp.sum(ma * qb - mb * qa, axis=0)
            same = jnp.sum(mc * qc, axis=0)
            cross = jnp.sum(ms * qc, axis=0)
            oc = jnp.where(low, same + pltpu.roll(same, 64, 1), cross - pltpu.roll(cross, 64, 1))
            summed = jnp.concatenate([oa, ob, oc], axis=1)
            damped.append(v - STEP * (summed - first_image[s]))

        parts = [unpack(damped[s]) for s in range(2)]
        for side, top in enumerate((ROWS - 2, 0)):
            for s in range(2):
                for q in range(2):
                    for t in range(2):
                        for h in range(2):
                            row = 8 * t + 4 * h + 2 * s + q
                            strip_rows[side, row:row + 1, :] = parts[s][q][t][top + h:top + h + 1]
            strip_out[turn, side] = strip_rows[side].astype(BF16)
        strips = []
        for i, (dc, ds) in enumerate(STRIPS):
            peer = (lax.rem(coil + dc + n, n), lax.rem(sect + ds + sections, sections))
            copy = pltpu.make_async_remote_copy(
                src_ref=strip_out.at[turn, 0 if dc > 0 else 1], dst_ref=strip_in.at[turn, i],
                send_sem=strip_send.at[turn, i], recv_sem=strip_recv.at[turn, i],
                device_id=peer, device_id_type=MESH,
            )
            if ds == 0 and i == 4:
                edge_out[turn] = jnp.concatenate(damped, axis=0).astype(BF16)
                sides = []
                for k, step in enumerate((1, -1)):
                    across = pltpu.make_async_remote_copy(
                        src_ref=edge_out.at[turn], dst_ref=edge_in.at[turn, k],
                        send_sem=edge_send.at[turn, k], recv_sem=edge_recv.at[turn, k],
                        device_id=(coil, lax.rem(sect + step + sections, sections)), device_id_type=MESH,
                    )
                    across.start()
                    sides.append(across)
            copy.start()
            strips.append(copy)

        def place_slices(values, ds):
            for s in range(2):
                for q in range(2):
                    for t in range(2):
                        grid_rows[t, pl.ds(32 + 2 * (2 + 2 * ds + s) + q, ROWS, stride=16), :] = values[s][q][t]

        def halve(first, last):
            rows = jnp.concatenate([grid_rows[0, first:last], grid_rows[1, first:last]], axis=1)
            grid_half[0, first:last] = pltpu.roll(rows, 1, 1).astype(BF16)
            grid_half[1, first:last] = rows.astype(BF16)
            grid_half[2, first:last] = pltpu.roll(rows, 255, 1).astype(BF16)

        def hidden_of(r):
            taps = jnp.concatenate([grid_half[e, 16 * r:16 * r + 48, :] for e in range(3)], axis=0)
            return jnp.maximum(dot(weight1[...], taps), 0.0).astype(BF16)

        def spots_of(r, hidden):
            spots = jnp.where(lanes_in, dot(weight2[...], hidden), 0.0)
            if r == 0:
                spots = jnp.where(coil > 0, spots, 0.0)
            if r == ROWS + 1:
                spots = jnp.where(coil < n - 1, spots, 0.0)
            return spots

        place_slices(parts, 0)
        if turn == 0:
            for copy in copies1 + copies2 + copies3:
                copy.wait_send()

            def wait_sent(d, carry):
                maps_copy(d).wait_send()
                return carry

            lax.fori_loop(1, n, wait_sent, 0)
        for k, step in enumerate((1, -1)):
            sides[k].wait_recv()
            inside = jnp.logical_and(sect - step >= 0, sect - step < sections)
            block = jnp.where(inside, edge_in[turn, k].astype(F32), 0.0)
            place_slices([unpack(block[0:ROWS]), unpack(block[ROWS:2 * ROWS])], -step)
        halve(32, 160)
        hidden = {r: hidden_of(r) for r in range(2, ROWS)}
        spots = {r: spots_of(r, hidden[r]) for r in range(2, ROWS)}

        for i, (dc, ds) in reversed(list(enumerate(STRIPS))):
            strips[i].wait_recv()
            inside = jnp.logical_and(
                jnp.logical_and(coil - dc >= 0, coil - dc < n),
                jnp.logical_and(sect - ds >= 0, sect - ds < sections),
            )
            block = jnp.where(inside, strip_in[turn, i].astype(F32), 0.0)
            for t in range(2):
                for h in range(2):
                    to = (0 if dc > 0 else 160) + 16 * h + 2 * (2 - 2 * ds)
                    grid_rows[t, to:to + 4, :] = block[8 * t + 4 * h:8 * t + 4 * h + 4]
        halve(0, 32)
        halve(160, 192)
        hidden = {r: hidden_of(r) for r in (0, 1, ROWS, ROWS + 1)}
        for r in hidden:
            spots[r] = spots_of(r, hidden[r])

        for r in range(ROWS):
            taps = spots[r][0:24] + spots[r + 1][24:48] + spots[r + 2][48:72]
            update = pltpu.roll(taps[0:8], 1, 1) + taps[8:16] + pltpu.roll(taps[16:24], 255, 1) + bias_rows
            for t in range(2):
                result[t, 4 * r:4 * r + 4, :] = update[0:4, 128 * t:128 * t + 128]
        for copy in sides + strips:
            copy.wait_send()

        image = []
        for s in range(2):
            update = [[result[t, pl.ds(2 * s + q, ROWS, stride=4), :] for t in range(2)] for q in range(2)]
            if turn < ITERS - 1:
                image.append(damped[s] + pack(*update))
            else:
                for q, value in enumerate(parts[s]):
                    for t in range(2):
                        result[t, pl.ds(2 * s + q, ROWS, stride=4), :] = value[t] + update[q][t]

    for r in range(ROWS):
        for s in range(2):
            rows = slice(4 * r + 2 * s, 4 * r + 2 * s + 2)
            out_ref[r, s, :, 0:128] = result[0, rows]
            out_ref[r, s, :, 128:W] = result[1, rows, 0:W - 128]


def per_device(n, sections, measured, coil_maps, sampling, conv_first, bias_first, conv_second, bias_second):
    height = measured.shape[0]
    by_columns = lambda t: t.transpose(1, 2, 3, 4, 0).reshape(2, 2 * W, height)
    consts = [jnp.asarray(t) for t in tables(height)]
    chips = n // 2
    x_size = min(X_CHIPS, chips // 2)
    z_size = chips // x_size
    dma = pltpu.SemaphoreType.DMA
    out = pl.pallas_call(
        lambda *refs: kernel(n, sections, *refs),
        out_shape=pltpu.VMEM((ROWS, 2, 2, W), F32),
        in_specs=[pl.BlockSpec(memory_space=pl.ANY)] * 14,
        out_specs=pl.BlockSpec(memory_space=pltpu.VMEM),
        scratch_shapes=[
            pltpu.VMEM((2, 384, height), F32),
            pltpu.VMEM((2, 384, height), F32),
            pltpu.VMEM((2, W), jnp.int32),
            pltpu.VMEM((384, 384), BF16),
            pltpu.VMEM((384, 384), BF16),
            pltpu.VMEM((height, 2 * height), BF16),
            pltpu.VMEM((height, 2 * height), BF16),
            pltpu.VMEM((54, CH), BF16),
            pltpu.VMEM((1, CH), F32),
            pltpu.VMEM((54, CH), BF16),
            pltpu.VMEM((1, 2), F32),
            pltpu.VMEM((4, 54, 144), BF16),
            pltpu.VMEM((4, 72, 54), BF16),
            pltpu.VMEM((CH, 256), BF16),
            pltpu.VMEM((2, 384, 1152), BF16),
            pltpu.VMEM((2, 768, 384), BF16),
            pltpu.VMEM((n, 2 * ROWS, 384), BF16),
            pltpu.VMEM((n, 2 * ROWS, 384), BF16),
            pltpu.VMEM((2, n, ROWS, 384), F32),
            pltpu.VMEM((2, n, ROWS, 128), F32),
            pltpu.VMEM((2, chips, 2, ROWS, 384), F32),
            pltpu.VMEM((2, chips, ROWS, 384), F32),
            pltpu.VMEM((2, z_size, x_size, ROWS, 384), F32),
            pltpu.VMEM((2, x_size - 1, z_size, ROWS, 384), F32),
            pltpu.VMEM((2, z_size, ROWS, 384), F32),
            pltpu.VMEM((2, z_size - 1, ROWS, 384), F32),
            pltpu.VMEM((256, 144), BF16),
            pltpu.VMEM((72, 256), BF16),
            pltpu.VMEM((ITERS, 2 * ROWS, 384), BF16),
            pltpu.VMEM((ITERS, 2, 2 * ROWS, 384), BF16),
            pltpu.VMEM((2, 16, 128), F32),
            pltpu.VMEM((ITERS, 2, 16, 128), BF16),
            pltpu.VMEM((ITERS, 6, 16, 128), BF16),
            pltpu.VMEM((2, 192, 128), F32),
            pltpu.VMEM((3, 192, 256), BF16),
            pltpu.VMEM((2, 4 * ROWS, 128), F32),
            dma((14,)),
            dma((n,)),
            dma((n,)),
            dma((2,)),
            dma((2,)),
            dma((2, x_size - 1)),
            dma((2, x_size - 1)),
            dma((2, z_size - 1)),
            dma((2, z_size - 1)),
            dma((ITERS, 2)),
            dma((ITERS, 2)),
            dma((ITERS, 6)),
            dma((ITERS, 6)),
        ],
        compiler_params=pltpu.CompilerParams(
            collective_id=0, has_side_effects=True, vmem_limit_bytes=60 * 1024 * 1024
        ),
        name="reconstruct",
    )(
        by_columns(measured), by_columns(coil_maps), sampling, *consts[:4],
        conv_first.T, bias_first.reshape(1, CH), conv_second, bias_second.reshape(1, 2), *consts[4:],
    )
    return out


def solution(mesh):
    n, sections = mesh.shape["coil"], mesh.shape["sect"]
    split = P(None, "coil", "sect", None, None)
    return jax.shard_map(
        lambda *args: per_device(n, sections, *args),
        mesh=mesh,
        in_specs=(split, split, P("sect", None), P(), P(), P(), P()),
        out_specs=P("coil", "sect", None, None),
        check_vma=False,
    )
```

```python
import math

import jax
import jax.numpy as jnp
import ml_dtypes
import numpy as np
from jax import lax
from jax.experimental import pallas as pl
from jax.experimental.pallas import tpu as pltpu
from jax.sharding import PartitionSpec as P

ITERS = 2
STEP = 0.5
X_CHIPS = 4
W = 192
CH = 64
BIAS_TAP = 48 + 16 + 12
ROWS = 8
F32 = jnp.float32
BF16 = jnp.bfloat16
MESH = pl.DeviceIdType.MESH

PACKED = np.concatenate([np.arange(0, 128), np.arange(192, 320), np.arange(128, 192), np.arange(320, 384)])
STRIPS = [(1, 1), (1, -1), (-1, 1), (-1, -1), (1, 0), (-1, 0)]


def split_halves(table):
    high = table.astype(ml_dtypes.bfloat16)
    low = (table - high.astype(np.float64)).astype(ml_dtypes.bfloat16)
    return high, low


def dft(length):
    index = np.arange(length)
    angle = (index[:, None] * index[None, :] % length) * (2.0 * math.pi / length)
    return np.cos(angle) / math.sqrt(length), np.sin(angle) / math.sqrt(length)


def tables(height):
    cosine, sine = dft(W)
    column = np.block([[cosine, -sine], [sine, cosine]])[PACKED][:, PACKED]
    cosine, sine = dft(height)
    row = np.concatenate([cosine, sine], axis=1)
    pick_first = np.zeros((4, 54, 144), np.float32)
    pick_second = np.zeros((4, 72, 54), np.float32)
    for a in range(3):
        for b in range(3):
            for e in range(3):
                for q in range(2):
                    tap = 2 * (9 * a + 3 * b + e) + q
                    for s in range(4):
                        pick_first[s, tap, 48 * e + 16 * a + 2 * (s + b) + q] = 1.0
                        if 0 <= s - b < 2:
                            pick_second[s, 24 * a + 8 * e + 2 * (s - b) + q, tap] = 1.0
    repeat = np.tile(np.eye(CH, dtype=np.float32), (1, 4))
    as_half = lambda t: t.astype(ml_dtypes.bfloat16)
    return split_halves(column) + split_halves(row) + (as_half(pick_first), as_half(pick_second), as_half(repeat))


def dot(a, b, dims=((1,), (0,))):
    return lax.dot_general(a, b, (dims, ((), ())), preferred_element_type=F32)


def halves(value):
    high = value.astype(BF16)
    return high, (value - high.astype(F32)).astype(BF16)


def pack_rows(value):
    return jnp.concatenate([value[0:128], value[192:320], value[128:192], value[320:384]], axis=0)


def low_lanes(shape):
    return lax.broadcasted_iota(jnp.int32, shape, len(shape) - 1) < 64


def unpack(value):
    third = value[:, 256:384]
    low = low_lanes(third.shape)
    real = (value[:, 0:128], jnp.where(low, third, 0.0))
    imag = (value[:, 128:256], jnp.where(low, pltpu.roll(third, 64, 1), 0.0))
    return real, imag


def pack(real, imag):
    third = jnp.where(low_lanes(real[1].shape), real[1], pltpu.roll(imag[1], 64, 1))
    return jnp.concatenate([real[0], imag[0], third], axis=1)


def kernel(n, sections, meas_hbm, maps_hbm, samp_hbm, th_hbm, tl_hbm, eh_hbm, el_hbm,
           first_hbm, bias_first_hbm, second_hbm, bias_second_hbm, pick_first_hbm, pick_second_hbm, repeat_hbm, out_ref,
           meas, maps, samp_ref, th, tl, eh, el,
           first_ref, bias_first_ref, second_ref, bias_second_ref, pick_first_ref, pick_second_ref, repeat_ref, masked, spread, outgoing, gathered, gathered_f, gathered_swap,
           part, got1, sum1, got2, sum2, got3, weight1, weight2, edge_out, edge_in, strip_rows, strip_out, strip_in, grid_rows, grid_half,
           result, load_sem, maps_send, maps_recv, rs1_send, rs1_recv, rs2_send, rs2_recv, rs3_send, rs3_recv,
           edge_send, edge_recv,
           strip_send, strip_recv):
    coil = lax.axis_index("coil")
    sect = lax.axis_index("sect")
    core = lax.rem(coil, 2)
    x_size = sum1.shape[2]
    z_size = sum1.shape[1]
    plane = 2 * x_size
    spot_in_plane = lax.rem(coil, plane)
    x = lax.rem(coil // 2, x_size)
    z = coil // plane

    loads = [
        pltpu.make_async_copy(src, dst, load_sem.at[i])
        for i, (src, dst) in enumerate(
            [
                (samp_hbm, samp_ref), (th_hbm, th), (tl_hbm, tl), (meas_hbm, meas), (eh_hbm, eh), (el_hbm, el),
                (maps_hbm, maps), (first_hbm, first_ref), (bias_first_hbm, bias_first_ref), (second_hbm, second_ref),
                (bias_second_hbm, bias_second_ref), (pick_first_hbm, pick_first_ref),
                (pick_second_hbm, pick_second_ref), (repeat_hbm, repeat_ref),
            ]
        )
    ]
    for load in loads[:7]:
        load.start()

    barrier = pltpu.get_barrier_semaphore()

    def greet(d, carry):
        pl.semaphore_signal(barrier, inc=1, device_id=(lax.rem(coil + d, n), sect), device_id_type=MESH)
        return carry

    lax.fori_loop(1, n, greet, 0)
    for dc in (-1, 0, 1):
        for ds in (-1, 1):
            peer = (lax.rem(coil + dc + n, n), lax.rem(sect + ds + sections, sections))
            pl.semaphore_signal(barrier, inc=1, device_id=peer, device_id_type=MESH)

    for load in loads[7:]:
        load.start()
    for load in loads[:3]:
        load.wait()
    flags = jnp.concatenate([samp_ref[...].astype(F32), jnp.zeros((2, 64), F32)], axis=1)
    flags = jnp.concatenate([flags, jnp.zeros((6, 256), F32)], axis=0).T
    table = jnp.concatenate([th[...], tl[...], th[...]], axis=1)

    for load in loads[3:7]:
        load.wait()
    copies1 = []
    columns = []
    for s in range(2):
        flag = flags[:, s:s + 1]
        flag = jnp.concatenate([flag[0:128], flag[0:128], flag[128:W], flag[128:W]], axis=0)
        xh, xl = halves(pack_rows(meas[s]) * flag)
        columns.append(dot(table, jnp.concatenate([xh, xh, xl], axis=0)))
    planes = []
    for s in range(2):
        zh, zl = halves(columns[s])
        planes.append(dot(jnp.concatenate([zh, zl, zh], axis=1), jnp.concatenate([eh[...], eh[...], el[...]], axis=0)))
    for s in range(2):
        both = planes[s]
        height = both.shape[1] // 2
        by_cos, by_sin = both[:, :height], both[:, height:]
        m = pack_rows(maps[s])
        terms = []
        for r0, i0, size in ((0, 128, 128), (256, 320, 64)):
            re, im = slice(r0, r0 + size), slice(i0, i0 + size)
            y_re = by_cos[re] - by_sin[im]
            y_im = by_cos[im] + by_sin[re]
            terms += [m[re] * y_re + m[im] * y_im, m[re] * y_im - m[im] * y_re]
        part[s] = jnp.concatenate(terms, axis=0).T.reshape(n // 2, 2, ROWS, 384)
        if s == 0:
            pl.semaphore_wait(barrier, n - 1 + 6)
        copy = pltpu.make_async_remote_copy(
            src_ref=part.at[s, :, 1 - core], dst_ref=got1.at[s], send_sem=rs1_send.at[s], recv_sem=rs1_recv.at[s],
            device_id=(coil + 1 - 2 * core, sect), device_id_type=MESH,
        )
        copy.start()
        copies1.append(copy)

    turned = [pack_rows(maps[s]).T.reshape(n, ROWS, 384) for s in range(2)]
    outgoing[...] = jnp.concatenate(turned, axis=1).astype(BF16)
    gathered[coil] = outgoing[coil]

    def maps_copy(d):
        peer = lax.rem(z + d // plane, z_size) * plane + lax.rem(spot_in_plane + d, plane)
        return pltpu.make_async_remote_copy(
            src_ref=outgoing.at[peer], dst_ref=gathered.at[coil], send_sem=maps_send.at[d], recv_sem=maps_recv.at[d],
            device_id=(peer, sect), device_id_type=MESH,
        )

    def send_maps(d, carry):
        maps_copy(d).start()
        return carry

    def send_far(d, carry):
        maps_copy(plane + lax.rem(d, n - plane)).start()
        return carry

    lax.fori_loop(plane, n, send_far, 0)

    copies2 = {}
    for s in range(2):
        copies1[s].wait_recv()
        sum1[s] = (part[s, :, core] + got1[s]).reshape(z_size, x_size, ROWS, 384)
        for d in [x_size // 2] + [i for i in range(1, x_size) if i != x_size // 2]:
            to = lax.rem(x + d, x_size)
            copy = pltpu.make_async_remote_copy(
                src_ref=sum1.at[s, :, to], dst_ref=got2.at[s, d - 1],
                send_sem=rs2_send.at[s, d - 1], recv_sem=rs2_recv.at[s, d - 1],
                device_id=((z * x_size + to) * 2 + core, sect), device_id_type=MESH,
            )
            copy.start()
            copies2[s, d] = copy

    lax.fori_loop(1, plane, send_maps, 0)
    for s in range(2):
        mask = samp_ref[s:s + 1, :].astype(F32)
        mask = jnp.concatenate([mask, jnp.zeros((1, 64), F32)], axis=1)
        tail = mask[:, 128:256]
        mask = jnp.concatenate([mask[:, 0:128], mask[:, 0:128], tail + pltpu.roll(tail, 64, 1)], axis=1)
        high = (th[...].astype(F32) * mask).astype(BF16)
        masked[s, :, 0:384] = high
        masked[s, :, 384:768] = (tl[...].astype(F32) * mask).astype(BF16)
        masked[s, :, 768:1152] = high
    for s in range(2):
        last = ((1,), (1,))
        mh, ml = masked[s, :, 0:384], masked[s, :, 384:768]
        high, low = halves(dot(masked[s], jnp.concatenate([mh, mh, ml], axis=1), last))
        spread[s, 0:384] = high
        spread[s, 384:768] = low

    copies3 = {}
    for s in range(2):
        total = sum1[s, :, x]
        for d in range(1, x_size):
            copies2[s, d].wait_recv()
            total = total + got2[s, d - 1]
        sum2[s] = total
        for d in [z_size // 2] + [i for i in range(1, z_size) if i != z_size // 2]:
            to = lax.rem(z + d, z_size)
            copy = pltpu.make_async_remote_copy(
                src_ref=sum2.at[s, to], dst_ref=got3.at[s, d - 1],
                send_sem=rs3_send.at[s, d - 1], recv_sem=rs3_recv.at[s, d - 1],
                device_id=((to * x_size + x) * 2 + core, sect), device_id_type=MESH,
            )
            copy.start()
            copies3[s, d] = copy

    for load in loads[7:]:
        load.wait()
    repeated = dot(second_ref[...], repeat_ref[...]).astype(BF16)
    of_slice = lax.broadcasted_iota(jnp.int32, (72, 256), 1) // 64
    second = jnp.zeros((72, 256), F32)
    for s in range(4):
        inside = jnp.logical_and(2 * sect - 1 + s >= 0, 2 * sect - 1 + s < 2 * sections)
        block = dot(pick_second_ref[s], repeated)
        second = second + jnp.where(jnp.logical_and(of_slice == s, inside), block, 0.0)
    weight2[...] = second.astype(BF16)
    diagonal = lax.broadcasted_iota(jnp.int32, (64, 64), 0) == lax.broadcasted_iota(jnp.int32, (64, 64), 1)
    bias_column = jnp.sum(jnp.where(diagonal, bias_first_ref[...], 0.0), axis=1, keepdims=True)
    bias_high = bias_column.astype(BF16).astype(F32)
    bias_rest = bias_column - bias_high
    bias_middle = bias_rest.astype(BF16).astype(F32)
    spot = lax.broadcasted_iota(jnp.int32, (64, 144), 1)
    bias_taps = jnp.where(spot == BIAS_TAP, bias_high, 0.0)
    bias_taps = jnp.where(spot == BIAS_TAP + 1, bias_middle, bias_taps)
    bias_taps = jnp.where(spot == BIAS_TAP + 2, bias_rest - bias_middle, bias_taps)
    for s in range(4):
        block = dot(first_ref[...], pick_first_ref[s], ((0,), (0,)))
        weight1[64 * s:64 * s + 64] = (block + bias_taps).astype(BF16)
    place = lax.rem(lax.broadcasted_iota(jnp.int32, (192, 128), 0), 16)
    for t in range(2):
        grid_rows[t] = jnp.where(jnp.logical_and(place >= 12, place < 15), 1.0, 0.0)

    def wait_maps(d, carry):
        maps_copy(d).wait_recv()
        return carry

    lax.fori_loop(1, n, wait_maps, 0)
    every = gathered[...].astype(F32)
    for s in range(2):
        mine = every[:, ROWS * s:ROWS * s + ROWS, :]
        gathered_f[s] = mine
        gathered_swap[s] = pltpu.roll(mine[:, :, 256:384].reshape(n * ROWS, 128), 64, 1).reshape(n, ROWS, 128)

    first_image = []
    for s in range(2):
        total = sum2[s, z]
        for d in range(1, z_size):
            copies3[s, d].wait_recv()
            total = total + got3[s, d - 1]
        first_image.append(total)

    lane = lax.broadcasted_iota(jnp.int32, (ROWS, 128), 1)
    low = lane < 64
    lanes_in = lax.broadcasted_iota(jnp.int32, (72, 256), 1) < W
    row_of_8 = lax.broadcasted_iota(jnp.int32, (ROWS, 256), 0)
    bias_rows = jnp.where(lax.rem(row_of_8, 2) == 0, bias_second_ref[0:1, 0:1], bias_second_ref[0:1, 1:2])
    image = first_image
    for turn in range(ITERS):
        damped = []
        products = []
        for s in range(2):
            v = image[s]
            va, vb, vc = v[None, :, 0:128], v[None, :, 128:256], v[:, 256:384]
            turned_c = pltpu.roll(vc, 64, 1)
            v_re = jnp.where(low, vc, turned_c)[None]
            v_im = jnp.where(low, -turned_c, vc)[None]
            ma, mb, mc = gathered_f[s, :, :, 0:128], gathered_f[s, :, :, 128:256], gathered_f[s, :, :, 256:384]
            ms = gathered_swap[s]
            pieces = [ma * va - mb * vb, ma * vb + mb * va, mc * v_re + ms * v_im]
            product = jnp.concatenate([p.reshape(n * ROWS, 128) for p in pieces], axis=1).astype(BF16)
            products.append(product)
        backs = [dot(jnp.concatenate([p, p], axis=1), spread[s]) for s, p in enumerate(products)]
        for s in range(2):
            v = image[s]
            back = backs[s].reshape(n, ROWS, 384)
            ma, mb, mc = gathered_f[s, :, :, 0:128], gathered_f[s, :, :, 128:256], gathered_f[s, :, :, 256:384]
            ms = gathered_swap[s]
            qa, qb, qc = back[:, :, 0:128], back[:, :, 128:256], back[:, :, 256:384]
            oa = jnp.sum(ma * qa + mb * qb, axis=0)
            ob = jnp.sum(ma * qb - mb * qa, axis=0)
            same = jnp.sum(mc * qc, axis=0)
            cross = jnp.sum(ms * qc, axis=0)
            oc = jnp.where(low, same + pltpu.roll(same, 64, 1), cross - pltpu.roll(cross, 64, 1))
            summed = jnp.concatenate([oa, ob, oc], axis=1)
            damped.append(v - STEP * (summed - first_image[s]))

        parts = [unpack(damped[s]) for s in range(2)]
        for side, top in enumerate((ROWS - 2, 0)):
            for s in range(2):
                for q in range(2):
                    for t in range(2):
                        for h in range(2):
                            row = 8 * t + 4 * h + 2 * s + q
                            strip_rows[side, row:row + 1, :] = parts[s][q][t][top + h:top + h + 1]
            strip_out[turn, side] = strip_rows[side].astype(BF16)
        strips = []
        for i, (dc, ds) in enumerate(STRIPS):
            peer = (lax.rem(coil + dc + n, n), lax.rem(sect + ds + sections, sections))
            copy = pltpu.make_async_remote_copy(
                src_ref=strip_out.at[turn, 0 if dc > 0 else 1], dst_ref=strip_in.at[turn, i],
                send_sem=strip_send.at[turn, i], recv_sem=strip_recv.at[turn, i],
                device_id=peer, device_id_type=MESH,
            )
            if ds == 0 and i == 4:
                edge_out[turn] = jnp.concatenate(damped, axis=0).astype(BF16)
                sides = []
                for k, step in enumerate((1, -1)):
                    across = pltpu.make_async_remote_copy(
                        src_ref=edge_out.at[turn], dst_ref=edge_in.at[turn, k],
                        send_sem=edge_send.at[turn, k], recv_sem=edge_recv.at[turn, k],
                        device_id=(coil, lax.rem(sect + step + sections, sections)), device_id_type=MESH,
                    )
                    across.start()
                    sides.append(across)
            copy.start()
            strips.append(copy)

        def place_slices(values, ds):
            for s in range(2):
                for q in range(2):
                    for t in range(2):
                        grid_rows[t, pl.ds(32 + 2 * (2 + 2 * ds + s) + q, ROWS, stride=16), :] = values[s][q][t]

        def halve(first, last):
            rows = jnp.concatenate([grid_rows[0, first:last], grid_rows[1, first:last]], axis=1)
            grid_half[0, first:last] = pltpu.roll(rows, 1, 1).astype(BF16)
            grid_half[1, first:last] = rows.astype(BF16)
            grid_half[2, first:last] = pltpu.roll(rows, 255, 1).astype(BF16)

        def hidden_of(r):
            taps = jnp.concatenate([grid_half[e, 16 * r:16 * r + 48, :] for e in range(3)], axis=0)
            return jnp.maximum(dot(weight1[...], taps), 0.0).astype(BF16)

        def spots_of(r, hidden):
            spots = jnp.where(lanes_in, dot(weight2[...], hidden), 0.0)
            if r == 0:
                spots = jnp.where(coil > 0, spots, 0.0)
            if r == ROWS + 1:
                spots = jnp.where(coil < n - 1, spots, 0.0)
            return spots

        place_slices(parts, 0)
        if turn == 0:
            for copy in copies1 + list(copies2.values()) + list(copies3.values()):
                copy.wait_send()

            def wait_sent(d, carry):
                maps_copy(d).wait_send()
                return carry

            lax.fori_loop(1, n, wait_sent, 0)
        for k, step in enumerate((1, -1)):
            sides[k].wait_recv()
            inside = jnp.logical_and(sect - step >= 0, sect - step < sections)
            block = jnp.where(inside, edge_in[turn, k].astype(F32), 0.0)
            place_slices([unpack(block[0:ROWS]), unpack(block[ROWS:2 * ROWS])], -step)
        halve(32, 160)
        hidden = {r: hidden_of(r) for r in range(2, ROWS)}
        spots = {r: spots_of(r, hidden[r]) for r in range(2, ROWS)}

        for i, (dc, ds) in reversed(list(enumerate(STRIPS))):
            strips[i].wait_recv()
            inside = jnp.logical_and(
                jnp.logical_and(coil - dc >= 0, coil - dc < n),
                jnp.logical_and(sect - ds >= 0, sect - ds < sections),
            )
            block = jnp.where(inside, strip_in[turn, i].astype(F32), 0.0)
            for t in range(2):
                for h in range(2):
                    to = (0 if dc > 0 else 160) + 16 * h + 2 * (2 - 2 * ds)
                    grid_rows[t, to:to + 4, :] = block[8 * t + 4 * h:8 * t + 4 * h + 4]
        halve(0, 32)
        halve(160, 192)
        hidden = {r: hidden_of(r) for r in (0, 1, ROWS, ROWS + 1)}
        for r in hidden:
            spots[r] = spots_of(r, hidden[r])

        for r in range(ROWS):
            taps = spots[r][0:24] + spots[r + 1][24:48] + spots[r + 2][48:72]
            update = pltpu.roll(taps[0:8], 1, 1) + taps[8:16] + pltpu.roll(taps[16:24], 255, 1) + bias_rows
            for t in range(2):
                result[t, 4 * r:4 * r + 4, :] = update[0:4, 128 * t:128 * t + 128]
        for copy in sides + strips:
            copy.wait_send()

        image = []
        for s in range(2):
            update = [[result[t, pl.ds(2 * s + q, ROWS, stride=4), :] for t in range(2)] for q in range(2)]
            if turn < ITERS - 1:
                image.append(damped[s] + pack(*update))
            else:
                for q, value in enumerate(parts[s]):
                    for t in range(2):
                        result[t, pl.ds(2 * s + q, ROWS, stride=4), :] = value[t] + update[q][t]

    for r in range(ROWS):
        for s in range(2):
            rows = slice(4 * r + 2 * s, 4 * r + 2 * s + 2)
            out_ref[r, s, :, 0:128] = result[0, rows]
            out_ref[r, s, :, 128:W] = result[1, rows, 0:W - 128]


def per_device(n, sections, measured, coil_maps, sampling, conv_first, bias_first, conv_second, bias_second):
    height = measured.shape[0]
    by_columns = lambda t: t.transpose(1, 2, 3, 4, 0).reshape(2, 2 * W, height)
    consts = [jnp.asarray(t) for t in tables(height)]
    chips = n // 2
    x_size = min(X_CHIPS, chips // 2)
    z_size = chips // x_size
    dma = pltpu.SemaphoreType.DMA
    out = pl.pallas_call(
        lambda *refs: kernel(n, sections, *refs),
        out_shape=pltpu.VMEM((ROWS, 2, 2, W), F32),
        in_specs=[pl.BlockSpec(memory_space=pl.ANY)] * 14,
        out_specs=pl.BlockSpec(memory_space=pltpu.VMEM),
        scratch_shapes=[
            pltpu.VMEM((2, 384, height), F32),
            pltpu.VMEM((2, 384, height), F32),
            pltpu.VMEM((2, W), jnp.int32),
            pltpu.VMEM((384, 384), BF16),
            pltpu.VMEM((384, 384), BF16),
            pltpu.VMEM((height, 2 * height), BF16),
            pltpu.VMEM((height, 2 * height), BF16),
            pltpu.VMEM((54, CH), BF16),
            pltpu.VMEM((1, CH), F32),
            pltpu.VMEM((54, CH), BF16),
            pltpu.VMEM((1, 2), F32),
            pltpu.VMEM((4, 54, 144), BF16),
            pltpu.VMEM((4, 72, 54), BF16),
            pltpu.VMEM((CH, 256), BF16),
            pltpu.VMEM((2, 384, 1152), BF16),
            pltpu.VMEM((2, 768, 384), BF16),
            pltpu.VMEM((n, 2 * ROWS, 384), BF16),
            pltpu.VMEM((n, 2 * ROWS, 384), BF16),
            pltpu.VMEM((2, n, ROWS, 384), F32),
            pltpu.VMEM((2, n, ROWS, 128), F32),
            pltpu.VMEM((2, chips, 2, ROWS, 384), F32),
            pltpu.VMEM((2, chips, ROWS, 384), F32),
            pltpu.VMEM((2, z_size, x_size, ROWS, 384), F32),
            pltpu.VMEM((2, x_size - 1, z_size, ROWS, 384), F32),
            pltpu.VMEM((2, z_size, ROWS, 384), F32),
            pltpu.VMEM((2, z_size - 1, ROWS, 384), F32),
            pltpu.VMEM((256, 144), BF16),
            pltpu.VMEM((72, 256), BF16),
            pltpu.VMEM((ITERS, 2 * ROWS, 384), BF16),
            pltpu.VMEM((ITERS, 2, 2 * ROWS, 384), BF16),
            pltpu.VMEM((2, 16, 128), F32),
            pltpu.VMEM((ITERS, 2, 16, 128), BF16),
            pltpu.VMEM((ITERS, 6, 16, 128), BF16),
            pltpu.VMEM((2, 192, 128), F32),
            pltpu.VMEM((3, 192, 256), BF16),
            pltpu.VMEM((2, 4 * ROWS, 128), F32),
            dma((14,)),
            dma((n,)),
            dma((n,)),
            dma((2,)),
            dma((2,)),
            dma((2, x_size - 1)),
            dma((2, x_size - 1)),
            dma((2, z_size - 1)),
            dma((2, z_size - 1)),
            dma((ITERS, 2)),
            dma((ITERS, 2)),
            dma((ITERS, 6)),
            dma((ITERS, 6)),
        ],
        compiler_params=pltpu.CompilerParams(
            collective_id=0, has_side_effects=True, vmem_limit_bytes=60 * 1024 * 1024
        ),
        name="reconstruct",
    )(
        by_columns(measured), by_columns(coil_maps), sampling, *consts[:4],
        conv_first.T, bias_first.reshape(1, CH), conv_second, bias_second.reshape(1, 2), *consts[4:],
    )
    return out


def solution(mesh):
    n, sections = mesh.shape["coil"], mesh.shape["sect"]
    split = P(None, "coil", "sect", None, None)
    return jax.shard_map(
        lambda *args: per_device(n, sections, *args),
        mesh=mesh,
        in_specs=(split, split, P("sect", None), P(), P(), P(), P()),
        out_specs=P("coil", "sect", None, None),
        check_vma=False,
    )
```
